512 devices in a mesh: dp: 64 (over x_lo, z, core), head: 8 (over x_hi, y).
Axes of the slice: x: 4 (x_hi: 2, x_lo: 2; x = x_hi * 2 + x_lo), y: 4, z: 16, core: 2. Of those that a mesh axis runs over, the one named last changes fastest.
Arguments:
- q_in: bfloat16 [65536, 3072], P(('dp', 'head'))
- k_in: bfloat16 [65536, 3072], P(('dp', 'head'))
- v_in: bfloat16 [65536, 3072], P(('dp', 'head')), may hold values from -6 to 6
- grad_out: bfloat16 [65536, 3072], P(('dp', 'head')), may hold values from -6 to 6
- q_gain: float32 [3072], replicated, may hold values from 0.5 to 2
- k_gain: float32 [3072], replicated, may hold values from 0.5 to 2
- res_len: int32 [64], replicated, may hold values from 1 to 960, as said below
- move_len: int32 [64], replicated, may hold values from 1 to 64, as said below
- step_index: int32 [64, 2], replicated, may hold values from 0 to 999
- dest_group: int32 [64], replicated, may hold values from 0 to 63, each once
- loss_weight: float32 [1000], replicated, may hold values from 0.25 to 4
Outputs:
- grad_q: bfloat16 [65536, 3072], P(('dp', 'head'))
- grad_k: bfloat16 [65536, 3072], P(('dp', 'head'))
- grad_q_gain: float32 [3072], P('head')
- grad_k_gain: float32 [3072], P('head')
The draws below stay inside these ranges and needn't reach their ends.
Inputs may be any that keep to these rules, and one draw needn't show every extreme that they name: `res_len`: staying clip lengths; some group's clip fills all 8 * 120 slots. `move_len`: leaving clip lengths; some group's clip fills all 8 * 8 slots. `dest_group`: A permutation of the groups.
All inputs are finite; a program needn't handle non-finite values.
Results may differ from the reference program's by a relative error of at most 0.009.
The reference program's roundings to bfloat16 on the way count: a program that leaves them out, or rounds other values in their place, can miss the bound.
Values may be sent and summed in bfloat16 or wider, within the bound.
No kernel may reach another device: no remote copies, remote signals or barrier semaphores. Data moves between devices by JAX's collectives and lax.ppermute only.
A program may use at most 64 MiB of HBM per device.

```python
import math
import jax
import jax.numpy as jnp
from jax import lax

HEAD_DIM = 128
TOK_DEV = 128
MOV = 8
NSTEPS = 1000
HD = 3072
RES = 120
TOKENS = 65536
N_DP = 64
N_HEAD = 8


def draw_q_in(key, part):
    key = jax.random.fold_in(key, 11)
    own = jax.random.normal(key, (TOKENS, HD), jnp.float32)
    return jnp.clip(own, -8.0, 8.0).astype(jnp.bfloat16)


def draw_k_in(key, part):
    key = jax.random.fold_in(key, 12)
    own = jax.random.normal(key, (TOKENS, HD), jnp.float32)
    return jnp.clip(own, -8.0, 8.0).astype(jnp.bfloat16)


def draw_res_len(key, part):
    key = jax.random.fold_in(key, 3)
    first_key, second_key = jax.random.split(key)
    drawn = jax.random.randint(first_key, (N_DP,), 1, RES * N_HEAD + 1)
    chosen = jax.random.randint(second_key, (), 0, N_DP)
    return jnp.where(jnp.arange(N_DP) == chosen, RES * N_HEAD, drawn).astype(jnp.int32)


def draw_move_len(key, part):
    key = jax.random.fold_in(key, 4)
    first_key, second_key = jax.random.split(key)
    drawn = jax.random.randint(first_key, (N_DP,), 1, MOV * N_HEAD + 1)
    chosen = jax.random.randint(second_key, (), 0, N_DP)
    return jnp.where(jnp.arange(N_DP) == chosen, MOV * N_HEAD, drawn).astype(jnp.int32)


def touch_ends(entries, key, smallest, largest):
    shape = entries.shape
    place = [jax.random.randint(jax.random.fold_in(key, axis), (), 0, shape[axis]) for axis in range(len(shape))]
    entries = entries.at[tuple(place)].set(smallest)
    longest = shape.index(max(shape))
    place[longest] = (place[longest] + 1) % shape[longest]
    return entries.at[tuple(place)].set(largest)


def levels(rng, extent, cuts, smallest, top_value):
    loudness, own = 1.0, jax.random.fold_in(rng, 6)
    for dim, shards_of in cuts:
        heights = jnp.exp(jax.random.uniform(jax.random.fold_in(own, dim), (shards_of,), jnp.float32, smallest / len(cuts), top_value / len(cuts)))
        loudness = loudness * jnp.repeat(heights, extent[dim] // shards_of).reshape([-1 if axis == dim else 1 for axis in range(len(extent))])
    return loudness


def noise(key, shape, deviation, reach, cuts=(), kind=jnp.bfloat16):
    array = deviation * jax.random.normal(key, shape, jnp.float32)
    if cuts:
        array = array * levels(key, shape, cuts, -0.22, 0.18)
    return jnp.clip(array, -reach, reach).astype(kind)


def setup_inputs(seed: int = 0) -> dict:
    key_list = jax.random.split(jax.random.key(seed), 12)
    q_in = draw_q_in(jax.random.fold_in(key_list[11], 71), 0)
    k_in = draw_k_in(jax.random.fold_in(key_list[11], 71), 0)
    v_in = noise(key_list[2], (TOKENS, HD), 1.0, 6.0, ((0, 512),))
    grad_out = noise(key_list[3], (TOKENS, HD), 1.0, 6.0, ((0, 512),))
    q_gain = jnp.clip(jnp.exp(jax.random.uniform(key_list[4], (HD,), jnp.float32, math.log(0.5), math.log(2.0))), 0.5, 2.0)
    k_gain = jnp.clip(jnp.exp(jax.random.uniform(key_list[5], (HD,), jnp.float32, math.log(0.5), math.log(2.0))), 0.5, 2.0)
    res_len = draw_res_len(jax.random.fold_in(key_list[11], 71), 0)
    move_len = draw_move_len(jax.random.fold_in(key_list[11], 71), 0)
    step_index = touch_ends(jax.random.randint(key_list[8], (N_DP, 2), 0, NSTEPS), jax.random.fold_in(key_list[8], 1), 0, NSTEPS - 1).astype(jnp.int32)
    dest_group = jax.random.permutation(key_list[9], N_DP).astype(jnp.int32)
    loss_weight = jnp.clip(jnp.exp(jax.random.uniform(key_list[10], (NSTEPS,), jnp.float32, math.log(0.25), math.log(4.0))), 0.25, 4.0)
    return dict(q_in=q_in, k_in=k_in, v_in=v_in, grad_out=grad_out, q_gain=q_gain, k_gain=k_gain, res_len=res_len, move_len=move_len, step_index=step_index, dest_group=dest_group, loss_weight=loss_weight)


EPS = 1e-06

def clip_grads(norm_query, norm_key, values, weighted, length, head_dim):
    row_count = norm_query.shape[0]
    head_count = norm_query.shape[1] // head_dim
    score_scale = 1.0 / math.sqrt(head_dim)
    key_live = jnp.arange(row_count, dtype=jnp.int32) < length

    def head_step(head_index, carried):
        query_grad, key_grad = carried
        offset = jnp.asarray(head_index, jnp.int32) * head_dim

        def take_head(block):
            return lax.dynamic_slice_in_dim(block, offset, head_dim, 1)
        queries, key_rows, value_rows, grad_rows = (take_head(norm_query), take_head(norm_key), take_head(values), take_head(weighted))
        scores = lax.dot_general(queries, key_rows, (((1,), (1,)), ((), ())), preferred_element_type=jnp.float32) * score_scale
        scores = jnp.where(key_live[None, :], scores, jnp.float32(-1e+30))
        row_max = lax.optimization_barrier(jnp.max(scores, axis=1, keepdims=True))
        raw_weights = jnp.exp(scores - row_max)
        weights = raw_weights / lax.optimization_barrier(jnp.sum(raw_weights, axis=1, keepdims=True))
        attended = jnp.dot(weights.astype(jnp.bfloat16), value_rows, preferred_element_type=jnp.float32)
        offset_term = lax.optimization_barrier(jnp.sum(grad_rows.astype(jnp.float32) * attended, axis=1, keepdims=True))
        weight_grad = lax.dot_general(grad_rows, value_rows, (((1,), (1,)), ((), ())), preferred_element_type=jnp.float32)
        score_grad = (weights * (weight_grad - offset_term)).astype(jnp.bfloat16)
        query_part = (jnp.dot(score_grad, key_rows, preferred_element_type=jnp.float32) * score_scale).astype(jnp.bfloat16)
        key_part = (lax.dot_general(score_grad, queries, (((0,), (0,)), ((), ())), preferred_element_type=jnp.float32) * score_scale).astype(jnp.bfloat16)
        query_grad = lax.dynamic_update_slice_in_dim(query_grad, query_part, offset, 1)
        key_grad = lax.dynamic_update_slice_in_dim(key_grad, key_part, offset, 1)
        return (query_grad, key_grad)
    zero_block = jnp.zeros(norm_query.shape, jnp.bfloat16)
    return lax.fori_loop(0, head_count, head_step, (zero_block, zero_block))

def reference(q_in, k_in, v_in, grad_out, q_gain, k_gain, res_len, move_len, step_index, dest_group, loss_weight):
    groups = jnp.arange(N_DP, dtype=jnp.int32)
    source = lax.optimization_barrier(jnp.sum(jnp.where(dest_group[:, None] == groups[None, :], groups[:, None], 0), axis=0)).astype(jnp.int32)

    def arrive(block):
        shaped = block.reshape(N_DP, N_HEAD, TOK_DEV, HD)
        return jnp.concatenate([shaped[:, :, :RES], shaped[source][:, :, RES:]], axis=2)
    q_dest, k_dest, v_dest = (arrive(q_in), arrive(k_in), arrive(v_in))
    grad_dest = grad_out.reshape(N_DP, N_HEAD, TOK_DEV, HD)
    move_here = move_len[source]
    weight_stay = loss_weight[step_index[:, 0]]
    weight_move = loss_weight[step_index[source, 1]]

    def per_group(inputs):
        queries, key_rows, value_rows, grad_rows, stay_len, leave_len, stay_weight, leave_weight = inputs
        q_float = queries.astype(jnp.float32)
        k_float = key_rows.astype(jnp.float32)
        q_scale = lax.rsqrt(lax.optimization_barrier(jnp.mean(q_float * q_float, axis=-1, keepdims=True)) + EPS)
        k_scale = lax.rsqrt(lax.optimization_barrier(jnp.mean(k_float * k_float, axis=-1, keepdims=True)) + EPS)
        norm_q = (q_float * q_scale * q_gain).astype(jnp.bfloat16)
        norm_k = (k_float * k_scale * k_gain).astype(jnp.bfloat16)
        slots = jnp.arange(N_HEAD, dtype=jnp.int32)[:, None]
        rows = jnp.arange(TOK_DEV, dtype=jnp.int32)[None, :]
        stay_pos = slots * RES + rows
        move_pos = slots * MOV + rows - RES
        token_weight = jnp.where(rows < RES, jnp.where(stay_pos < stay_len, stay_weight, jnp.float32(0.0)), jnp.where(move_pos < leave_len, leave_weight, jnp.float32(0.0)))
        weighted = (grad_rows.astype(jnp.float32) * token_weight[:, :, None]).astype(jnp.bfloat16)

        def split_clips(block):
            return (block[:, :RES].reshape(N_HEAD * RES, HD), block[:, RES:].reshape(N_HEAD * MOV, HD))
        pieces = [split_clips(block) for block in (norm_q, norm_k, value_rows, weighted)]
        stay_query, stay_key = clip_grads(pieces[0][0], pieces[1][0], pieces[2][0], pieces[3][0], stay_len, HEAD_DIM)
        move_query, move_key = clip_grads(pieces[0][1], pieces[1][1], pieces[2][1], pieces[3][1], leave_len, HEAD_DIM)

        def join_clips(staying, moving):
            return jnp.concatenate([staying.reshape(N_HEAD, RES, HD), moving.reshape(N_HEAD, MOV, HD)], axis=1)
        grad_qn = join_clips(stay_query, move_query).astype(jnp.float32)
        grad_kn = join_clips(stay_key, move_key).astype(jnp.float32)
        dots_q = lax.optimization_barrier(jnp.sum(q_float * q_gain * grad_qn, axis=-1, keepdims=True))
        dots_k = lax.optimization_barrier(jnp.sum(k_float * k_gain * grad_kn, axis=-1, keepdims=True))
        out_q = (q_scale * (q_gain * grad_qn) - q_float * (q_scale * q_scale * q_scale) * dots_q / HD).astype(jnp.bfloat16)
        out_k = (k_scale * (k_gain * grad_kn) - k_float * (k_scale * k_scale * k_scale) * dots_k / HD).astype(jnp.bfloat16)
        gain_q = lax.optimization_barrier(jnp.sum(grad_qn * q_float * q_scale, axis=(0, 1)))
        gain_k = lax.optimization_barrier(jnp.sum(grad_kn * k_float * k_scale, axis=(0, 1)))
        return (out_q, out_k, gain_q, gain_k)
    out_q, out_k, gain_q, gain_k = lax.map(per_group, (q_dest, k_dest, v_dest, grad_dest, res_len, move_here, weight_stay, weight_move))
    return (out_q.reshape(TOKENS, HD), out_k.reshape(TOKENS, HD), lax.optimization_barrier(jnp.sum(gain_q, axis=0)), lax.optimization_barrier(jnp.sum(gain_k, axis=0)))
```

```python
import math

import jax
import jax.numpy as jnp
from jax import lax
from jax.experimental import pallas as pl
from jax.experimental.pallas import tpu as pltpu
from jax.sharding import PartitionSpec as P

HEAD_DIM = 128
TOK_DEV = 128
MOV = 8
RES = 120
EPS = 1e-06
WAYS = 8
GROUPS = 64
HD = 3072
LOCAL = HD // WAYS
HEADS = LOCAL // HEAD_DIM
BLOCKS = HD // 128
SCALE = 1.0 / math.sqrt(HEAD_DIM)
F32 = jnp.float32
BF16 = jnp.bfloat16
VMEM_LIMIT = 56 * 1024 * 1024

PLANE = [[xl * 32 + z * 2 + c for xl in range(2) for c in range(2)] for z in range(16)]
ZRING = [[xl * 32 + z * 2 + c for z in range(16)] for xl in range(2) for c in range(2)]

SMEM = pl.BlockSpec(memory_space=pltpu.SMEM)


def params(count=0):
    return pltpu.CompilerParams(
        vmem_limit_bytes=VMEM_LIMIT,
        dimension_semantics=("arbitrary",) * count if count else None,
    )


def find_source(dest_ref, group):
    return lax.fori_loop(
        0, GROUPS, lambda g, found: jnp.where(dest_ref[g] == group, g, found), jnp.int32(0)
    )


def pack_kernel(q_ref, k_ref, v_ref, out_ref):
    q = q_ref[...].astype(F32)[8:16]
    k = k_ref[...].astype(F32)[8:16]
    v = v_ref[...].astype(F32)[8:16]
    pair = jnp.concatenate([q, k], axis=0).astype(BF16)
    half = HD // 2
    tail = jnp.concatenate([v[:, :half], v[:, half:]], axis=0).astype(BF16)
    for c in range(BLOCKS):
        out_ref[c] = pair[:, c * 128 : (c + 1) * 128]
    for c in range(BLOCKS // 2):
        out_ref[BLOCKS + c] = tail[:, c * 128 : (c + 1) * 128]
    rest = GROUPS - BLOCKS - BLOCKS // 2
    out_ref[pl.ds(BLOCKS + BLOCKS // 2, rest)] = jnp.zeros((rest, 16, 128), BF16)


def pack_short(q_in, k_in, v_in):
    spec = pl.BlockSpec((16, HD), lambda i: (TOK_DEV // 16 - 1, 0))
    return pl.pallas_call(
        pack_kernel,
        grid=(1,),
        in_specs=[spec] * 3,
        out_specs=pl.BlockSpec((GROUPS, 16, 128), lambda i: (0, 0, 0)),
        out_shape=jax.ShapeDtypeStruct((GROUPS, 16, 128), BF16),
        compiler_params=params(1),
        name="pack_short",
    )(q_in, k_in, v_in)


def scatter_kernel(dest_ref, in_ref, out_ref):
    def step(g, carry):
        out_ref[dest_ref[g]] = in_ref[g]
        return carry

    lax.fori_loop(0, GROUPS, step, 0)


def scatter_short(dest_group, parts):
    whole = pl.BlockSpec(memory_space=pltpu.VMEM)
    return pl.pallas_call(
        scatter_kernel,
        in_specs=[SMEM, whole],
        out_specs=whole,
        out_shape=jax.ShapeDtypeStruct(parts.shape, BF16),
        compiler_params=params(),
        name="scatter_short",
    )(dest_group, parts)


def norm_rows(rows, gain):
    scale = lax.rsqrt(jnp.sum(rows * rows, axis=1, keepdims=True) / HD + EPS)
    return rows * scale * gain


def unpack_kernel(in_ref, qg_ref, kg_ref, send_ref, raw_ref):
    pair = jnp.concatenate([in_ref[c] for c in range(BLOCKS)], axis=1).astype(F32)
    tail = jnp.concatenate([in_ref[BLOCKS + c] for c in range(BLOCKS // 2)], axis=1).astype(F32)
    q, k = pair[0:8], pair[8:16]
    v = jnp.concatenate([tail[0:8], tail[8:16]], axis=1)
    qn = norm_rows(q, qg_ref[...])
    kn = norm_rows(k, kg_ref[...])
    zero = jnp.zeros((8, HD), F32)
    first = jnp.concatenate([qn, kn], axis=0).astype(BF16)
    second = jnp.concatenate([v, zero], axis=0).astype(BF16)
    for p in range(WAYS):
        send_ref[p, 0:16, :] = first[:, p * LOCAL : (p + 1) * LOCAL]
        send_ref[p, 16:32, :] = second[:, p * LOCAL : (p + 1) * LOCAL]
    raw_ref[0] = jnp.concatenate([zero, q], axis=0).astype(BF16)
    raw_ref[1] = jnp.concatenate([zero, k], axis=0).astype(BF16)


def unpack_short(parts, q_gain, k_gain):
    whole = pl.BlockSpec(memory_space=pltpu.VMEM)
    return pl.pallas_call(
        unpack_kernel,
        in_specs=[whole] * 3,
        out_specs=[whole] * 2,
        out_shape=[
            jax.ShapeDtypeStruct((WAYS, 32, LOCAL), BF16),
            jax.ShapeDtypeStruct((2, 16, HD), BF16),
        ],
        compiler_params=params(),
        name="unpack_short",
    )(parts, q_gain, k_gain)


PRE_ROWS = 32


def pre_kernel(
    dest_ref, res_ref, move_ref, step_ref, table_ref,
    q_ref, k_ref, v_ref, go_ref, qg_ref, kg_ref,
    *rest,
):
    outs, (qn_ref, kn_ref) = rest[:WAYS], rest[WAYS:]
    group = lax.axis_index("dp")
    slot = lax.axis_index("head")
    source = find_source(dest_ref, group)
    stay_weight = table_ref[step_ref[group, 0]]
    move_weight = table_ref[step_ref[source, 1]]
    rows = pl.program_id(0) * PRE_ROWS + lax.broadcasted_iota(jnp.int32, (PRE_ROWS, 1), 0)
    stay = jnp.where(slot * RES + rows < res_ref[group], stay_weight, 0.0)
    move = jnp.where(slot * MOV + rows - RES < move_ref[source], move_weight, 0.0)
    weight = jnp.where(rows < RES, stay, move)
    qn_ref[...] = norm_rows(q_ref[...].astype(F32), qg_ref[...]).astype(BF16)
    kn_ref[...] = norm_rows(k_ref[...].astype(F32), kg_ref[...]).astype(BF16)
    for s in range(WAYS):
        start = pl.multiple_of(jnp.bitwise_xor(slot, s) * LOCAL, 128)
        cols = pl.ds(start, LOCAL)
        outs[s][0] = qn_ref[:, cols]
        outs[s][1] = kn_ref[:, cols]
        outs[s][2] = v_ref[:, cols]
        outs[s][3] = (go_ref[:, cols].astype(F32) * weight).astype(BF16)


def prepare(dest, res_len, move_len, steps, table, q_in, k_in, v_in, grad_out, q_gain, k_gain):
    rows = pl.BlockSpec((PRE_ROWS, HD), lambda i: (i, 0))
    gain = pl.BlockSpec((1, HD), lambda i: (0, 0))
    return pl.pallas_call(
        pre_kernel,
        grid=(TOK_DEV // PRE_ROWS,),
        in_specs=[SMEM] * 5 + [rows] * 4 + [gain] * 2,
        out_specs=[pl.BlockSpec((4, PRE_ROWS, LOCAL), lambda i: (0, i, 0))] * WAYS,
        out_shape=[jax.ShapeDtypeStruct((4, TOK_DEV, LOCAL), BF16)] * WAYS,
        scratch_shapes=[pltpu.VMEM((PRE_ROWS, HD), BF16)] * 2,
        compiler_params=params(1),
        cost_estimate=pl.CostEstimate(flops=20_000_000, bytes_accessed=6_300_000, transcendentals=0),
        name="prepare",
    )(dest, res_len, move_len, steps, table, q_in, k_in, v_in, grad_out, q_gain, k_gain)


def nt(a, b):
    return lax.dot_general(a, b, (((1,), (1,)), ((), ())), preferred_element_type=F32)


def tn(a, b):
    return lax.dot_general(a, b, (((0,), (0,)), ((), ())), preferred_element_type=F32)


def grads(q, k, v, g, bias):
    scores = nt(q, k) * SCALE + bias
    top = jnp.max(scores, axis=1, keepdims=True)
    raw = jnp.exp(scores - top)
    weights = raw * (1.0 / jnp.sum(raw, axis=1, keepdims=True))
    attended = jnp.dot(weights.astype(BF16), v, preferred_element_type=F32)
    delta = jnp.sum(g.astype(F32) * attended, axis=1, keepdims=True)
    score_grad = (weights * (nt(g, v) - delta)).astype(BF16)
    query_grad = jnp.dot(score_grad, k, preferred_element_type=F32) * SCALE
    return query_grad, tn(score_grad, q)


QUERY_ROWS = 256
ALL = WAYS * TOK_DEV


def attention_kernel(dest_ref, res_ref, move_ref, *rest):
    slots, rest = rest[:WAYS], rest[WAYS:]
    short_ref, qg_ref, kg_ref, out_ref, gain_ref, q_ref, k_ref, v_ref, g_ref, dq_ref, dk_ref = rest
    head = pl.program_id(0)
    group = lax.axis_index("dp")
    slot = lax.axis_index("head")
    source = find_source(dest_ref, group)
    stay_len = res_ref[group]
    move_len = move_ref[source]
    live_rows = lax.broadcasted_iota(jnp.int32, (TOK_DEV, 1), 0) < RES
    lanes = lax.broadcasted_iota(jnp.int32, (1, TOK_DEV), 1)
    biases = []
    for s in range(WAYS):
        here = pl.ds(s * TOK_DEV, TOK_DEV)
        q_ref[here] = slots[s][0]
        k_ref[here] = slots[s][1]
        v_ref[here] = slots[s][2]
        g_ref[here] = jnp.where(live_rows, slots[s][3].astype(F32), 0.0).astype(BF16)
        peer = jnp.bitwise_xor(slot, s)
        limit = jnp.minimum(stay_len - peer * RES, RES)
        biases.append(jnp.where(lanes < limit, 0.0, -1e30).astype(F32))
    bias = jnp.concatenate(biases, axis=1)
    dk_ref[...] = jnp.zeros_like(dk_ref)

    def block(i, carry):
        here = pl.ds(pl.multiple_of(i * QUERY_ROWS, QUERY_ROWS), QUERY_ROWS)
        dq, dk = grads(q_ref[here], k_ref[...], v_ref[...], g_ref[here], bias)
        dq_ref[here] = dq
        dk_ref[...] += dk
        return carry

    lax.fori_loop(0, ALL // QUERY_ROWS, block, 0)

    peers = [jnp.bitwise_xor(slot, s) for s in range(WAYS)]
    lines = [short_ref[p].astype(F32) for p in peers]
    short_q = jnp.concatenate([x[0:8] for x in lines], axis=0).astype(BF16)
    short_k = jnp.concatenate([x[8:16] for x in lines], axis=0).astype(BF16)
    short_v = jnp.concatenate([x[16:24] for x in lines], axis=0).astype(BF16)
    short_g = jnp.concatenate(
        [slots[s][3, pl.ds(112, 16)].astype(F32)[8:16] for s in range(WAYS)], axis=0
    ).astype(BF16)
    lane = lax.broadcasted_iota(jnp.int32, (1, WAYS * MOV), 1)
    position = jnp.bitwise_xor(lane // MOV, slot) * MOV + lane % MOV
    short_bias = jnp.where(position < move_len, 0.0, -1e30).astype(F32)
    short_dq, short_dk = grads(short_q, short_k, short_v, short_g, short_bias)
    short_dq = short_dq.astype(BF16).astype(F32)
    short_dk = (short_dk * SCALE).astype(BF16).astype(F32)

    dq = dq_ref[...].astype(BF16)
    dk = (dk_ref[...] * SCALE).astype(BF16)
    for s in range(WAYS):
        for n, stay, short in ((0, dq, short_dq), (1, dk, short_dk)):
            rows = stay[s * TOK_DEV : (s + 1) * TOK_DEV].astype(F32)
            rows = jnp.concatenate([rows[:RES], short[s * MOV : (s + 1) * MOV]], axis=0)
            out_ref[peers[s], n] = rows.astype(BF16)

    def total(stay, norm, short, short_norm, gain_ref):
        summed = jnp.sum(stay.astype(F32) * norm.astype(F32), axis=0, keepdims=True)
        summed += jnp.sum(short * short_norm.astype(F32), axis=0, keepdims=True)
        return summed / gain_ref[pl.ds(slot * HEADS + head, 1)]

    gain_ref[pl.ds(head, 1)] = total(dq, q_ref[...], short_dq, short_q, qg_ref)
    gain_ref[pl.ds(HEADS + head, 1)] = total(dk, k_ref[...], short_dk, short_k, kg_ref)


def attention(dest, res_len, move_len, slots, short, q_gain, k_gain):
    whole = lambda shape: pl.BlockSpec(shape, lambda b: (0,) * len(shape))
    return pl.pallas_call(
        attention_kernel,
        grid=(HEADS,),
        in_specs=[SMEM] * 3
        + [pl.BlockSpec((4, TOK_DEV, 128), lambda b: (0, 0, b))] * WAYS
        + [pl.BlockSpec((WAYS, 32, 128), lambda b: (0, 0, b))]
        + [whole((BLOCKS, 128))] * 2,
        out_specs=[
            pl.BlockSpec((WAYS, 2, TOK_DEV, 128), lambda b: (0, 0, 0, b)),
            whole((8, 128)),
        ],
        out_shape=[
            jax.ShapeDtypeStruct((WAYS, 2, TOK_DEV, LOCAL), BF16),
            jax.ShapeDtypeStruct((8, 128), F32),
        ],
        scratch_shapes=[pltpu.VMEM((ALL, 128), BF16)] * 4 + [pltpu.VMEM((ALL, 128), F32)] * 2,
        compiler_params=params(1),
        cost_estimate=pl.CostEstimate(
            flops=4_000_000_000, bytes_accessed=5_000_000, transcendentals=3_200_000
        ),
        name="attention",
    )(dest, res_len, move_len, *slots, short, q_gain, k_gain)


POST_ROWS = 32


def post_kernel(q_ref, k_ref, raw_ref, qg_ref, kg_ref, dq_ref, dk_ref, oq_ref, ok_ref):
    last = pl.program_id(0) == TOK_DEV // POST_ROWS - 1
    row = lax.broadcasted_iota(jnp.int32, (POST_ROWS, 1), 0)
    use_short = jnp.logical_and(last, row >= POST_ROWS - MOV)

    def one(in_ref, which, gain_ref, grad_ref, out_ref):
        short = raw_ref[which].astype(F32)
        short = jnp.concatenate([jnp.zeros((POST_ROWS - 16, HD), F32), short], axis=0)
        x = jnp.where(use_short, short, in_ref[...].astype(F32))
        scale = lax.rsqrt(jnp.sum(x * x, axis=1, keepdims=True) / HD + EPS)
        gain = gain_ref[...]
        grad = jnp.concatenate([grad_ref[p, 0].astype(F32) for p in range(WAYS)], axis=1) * gain
        dots = jnp.sum(x * grad, axis=1, keepdims=True)
        out_ref[...] = (scale * grad - x * ((scale * scale * scale) * dots / HD)).astype(BF16)

    one(q_ref, 0, qg_ref, dq_ref, oq_ref)
    one(k_ref, 1, kg_ref, dk_ref, ok_ref)


def finish(q_in, k_in, raw, q_gain, k_gain, back):
    rows = pl.BlockSpec((POST_ROWS, HD), lambda i: (i, 0))
    gain = pl.BlockSpec((1, HD), lambda i: (0, 0))
    return pl.pallas_call(
        post_kernel,
        grid=(TOK_DEV // POST_ROWS,),
        in_specs=[
            rows,
            rows,
            pl.BlockSpec((2, 16, HD), lambda i: (0, 0, 0)),
            gain,
            gain,
            pl.BlockSpec((WAYS, 1, POST_ROWS, LOCAL), lambda i: (0, 0, i, 0)),
            pl.BlockSpec((WAYS, 1, POST_ROWS, LOCAL), lambda i: (0, 1, i, 0)),
        ],
        out_specs=[rows, rows],
        out_shape=[jax.ShapeDtypeStruct((TOK_DEV, HD), BF16)] * 2,
        compiler_params=params(1),
        cost_estimate=pl.CostEstimate(flops=20_000_000, bytes_accessed=4_800_000, transcendentals=0),
        name="finish",
    )(q_in, k_in, raw, q_gain, k_gain, back, back)


def swap_all(x, axis):
    return lax.all_to_all(x, axis, split_axis=0, concat_axis=0, tiled=True)


def gather_sum(x, rings):
    return jnp.sum(lax.all_gather(x, "dp", axis_index_groups=rings), axis=0)


def local(
    q_in, k_in, v_in, grad_out, q_gain, k_gain,
    res_len, move_len, step_index, dest_group, loss_weight,
):
    gain_q, gain_k = q_gain.reshape(1, HD), k_gain.reshape(1, HD)
    spread = swap_all(pack_short(q_in, k_in, v_in), "dp")
    own, *outgoing = prepare(
        dest_group, res_len, move_len, step_index, loss_weight,
        q_in, k_in, v_in, grad_out, gain_q, gain_k,
    )
    arrived = [own] + [
        lax.ppermute(x, "head", [(i, i ^ (n + 1)) for i in range(WAYS)])
        for n, x in enumerate(outgoing)
    ]
    routed = swap_all(scatter_short(dest_group, spread), "dp")
    short, raw = unpack_short(routed, gain_q, gain_k)
    short = swap_all(short, "head")
    grad, part = attention(
        dest_group, res_len, move_len, arrived, short,
        q_gain.reshape(BLOCKS, 128), k_gain.reshape(BLOCKS, 128),
    )
    back = swap_all(grad, "head")
    total = gather_sum(gather_sum(part, PLANE), ZRING)
    out_q, out_k = finish(q_in, k_in, raw, gain_q, gain_k, back)
    return (
        out_q,
        out_k,
        total[:HEADS].reshape(LOCAL),
        total[HEADS : 2 * HEADS].reshape(LOCAL),
    )


def solution(mesh):
    tokens = P(("dp", "head"), None)
    return jax.shard_map(
        local,
        mesh=mesh,
        in_specs=(tokens,) * 4 + (P(),) * 7,
        out_specs=(tokens, tokens, P("head"), P("head")),
        check_vma=False,
    )
```

```python
import math

import jax
import jax.numpy as jnp
from jax import lax
from jax.experimental import pallas as pl
from jax.experimental.pallas import tpu as pltpu
from jax.sharding import PartitionSpec as P

HEAD_DIM = 128
TOK_DEV = 128
MOV = 8
RES = 120
EPS = 1e-06
WAYS = 8
GROUPS = 64
HD = 3072
LOCAL = HD // WAYS
HEADS = LOCAL // HEAD_DIM
BLOCKS = HD // 128
SCALE = 1.0 / math.sqrt(HEAD_DIM)
F32 = jnp.float32
BF16 = jnp.bfloat16
VMEM_LIMIT = 56 * 1024 * 1024

PLANE = [[xl * 32 + z * 2 + c for xl in range(2) for c in range(2)] for z in range(16)]
ZRING = [[xl * 32 + z * 2 + c for z in range(16)] for xl in range(2) for c in range(2)]

SMEM = pl.BlockSpec(memory_space=pltpu.SMEM)


def params(count=0):
    return pltpu.CompilerParams(
        vmem_limit_bytes=VMEM_LIMIT,
        dimension_semantics=("arbitrary",) * count if count else None,
    )


def find_source(dest_ref, group):
    return lax.fori_loop(
        0, GROUPS, lambda g, found: jnp.where(dest_ref[g] == group, g, found), jnp.int32(0)
    )


def pack_kernel(q_ref, k_ref, v_ref, out_ref):
    q = q_ref[...].astype(F32)[8:16]
    k = k_ref[...].astype(F32)[8:16]
    v = v_ref[...].astype(F32)[8:16]
    pair = jnp.concatenate([q, k], axis=0).astype(BF16)
    half = HD // 2
    tail = jnp.concatenate([v[:, :half], v[:, half:]], axis=0).astype(BF16)
    for c in range(BLOCKS):
        out_ref[c] = pair[:, c * 128 : (c + 1) * 128]
    for c in range(BLOCKS // 2):
        out_ref[BLOCKS + c] = tail[:, c * 128 : (c + 1) * 128]
    rest = GROUPS - BLOCKS - BLOCKS // 2
    out_ref[pl.ds(BLOCKS + BLOCKS // 2, rest)] = jnp.zeros((rest, 16, 128), BF16)


def pack_short(q_in, k_in, v_in):
    spec = pl.BlockSpec((16, HD), lambda i: (TOK_DEV // 16 - 1, 0))
    return pl.pallas_call(
        pack_kernel,
        grid=(1,),
        in_specs=[spec] * 3,
        out_specs=pl.BlockSpec((GROUPS, 16, 128), lambda i: (0, 0, 0)),
        out_shape=jax.ShapeDtypeStruct((GROUPS, 16, 128), BF16),
        compiler_params=params(1),
        name="pack_short",
    )(q_in, k_in, v_in)


def scatter_kernel(dest_ref, in_ref, out_ref):
    def step(g, carry):
        out_ref[dest_ref[g]] = in_ref[g]
        return carry

    lax.fori_loop(0, GROUPS, step, 0)


def scatter_short(dest_group, parts):
    whole = pl.BlockSpec(memory_space=pltpu.VMEM)
    return pl.pallas_call(
        scatter_kernel,
        in_specs=[SMEM, whole],
        out_specs=whole,
        out_shape=jax.ShapeDtypeStruct(parts.shape, BF16),
        compiler_params=params(),
        name="scatter_short",
    )(dest_group, parts)


def norm_rows(rows, gain):
    scale = lax.rsqrt(jnp.sum(rows * rows, axis=1, keepdims=True) / HD + EPS)
    return rows * scale * gain


def unpack_kernel(in_ref, qg_ref, kg_ref, send_ref, raw_ref):
    pair = jnp.concatenate([in_ref[c] for c in range(BLOCKS)], axis=1).astype(F32)
    tail = jnp.concatenate([in_ref[BLOCKS + c] for c in range(BLOCKS // 2)], axis=1).astype(F32)
    q, k = pair[0:8], pair[8:16]
    v = jnp.concatenate([tail[0:8], tail[8:16]], axis=1)
    qn = norm_rows(q, qg_ref[...])
    kn = norm_rows(k, kg_ref[...])
    zero = jnp.zeros((8, HD), F32)
    first = jnp.concatenate([qn, kn], axis=0).astype(BF16)
    second = jnp.concatenate([v, zero], axis=0).astype(BF16)
    for p in range(WAYS):
        send_ref[p, 0:16, :] = first[:, p * LOCAL : (p + 1) * LOCAL]
        send_ref[p, 16:32, :] = second[:, p * LOCAL : (p + 1) * LOCAL]
    raw_ref[0] = jnp.concatenate([zero, q], axis=0).astype(BF16)
    raw_ref[1] = jnp.concatenate([zero, k], axis=0).astype(BF16)


def unpack_short(parts, q_gain, k_gain):
    whole = pl.BlockSpec(memory_space=pltpu.VMEM)
    return pl.pallas_call(
        unpack_kernel,
        in_specs=[whole] * 3,
        out_specs=[whole] * 2,
        out_shape=[
            jax.ShapeDtypeStruct((WAYS, 32, LOCAL), BF16),
            jax.ShapeDtypeStruct((2, 16, HD), BF16),
        ],
        compiler_params=params(),
        name="unpack_short",
    )(parts, q_gain, k_gain)


PRE_ROWS = 32


def pre_kernel(
    dest_ref, res_ref, move_ref, step_ref, table_ref,
    q_ref, k_ref, v_ref, go_ref, qg_ref, kg_ref,
    *rest,
):
    outs, (qn_ref, kn_ref) = rest[:WAYS], rest[WAYS:]
    group = lax.axis_index("dp")
    slot = lax.axis_index("head")
    source = find_source(dest_ref, group)
    stay_weight = table_ref[step_ref[group, 0]]
    move_weight = table_ref[step_ref[source, 1]]
    rows = pl.program_id(0) * PRE_ROWS + lax.broadcasted_iota(jnp.int32, (PRE_ROWS, 1), 0)
    stay = jnp.where(slot * RES + rows < res_ref[group], stay_weight, 0.0)
    move = jnp.where(slot * MOV + rows - RES < move_ref[source], move_weight, 0.0)
    weight = jnp.where(rows < RES, stay, move)
    qn_ref[...] = norm_rows(q_ref[...].astype(F32), qg_ref[...]).astype(BF16)
    kn_ref[...] = norm_rows(k_ref[...].astype(F32), kg_ref[...]).astype(BF16)
    for s in range(WAYS):
        start = pl.multiple_of(jnp.bitwise_xor(slot, s) * LOCAL, 128)
        cols = pl.ds(start, LOCAL)
        outs[s][0] = qn_ref[:, cols]
        outs[s][1] = kn_ref[:, cols]
        outs[s][2] = v_ref[:, cols]
        outs[s][3] = (go_ref[:, cols].astype(F32) * weight).astype(BF16)


def prepare(dest, res_len, move_len, steps, table, q_in, k_in, v_in, grad_out, q_gain, k_gain):
    rows = pl.BlockSpec((PRE_ROWS, HD), lambda i: (i, 0))
    gain = pl.BlockSpec((1, HD), lambda i: (0, 0))
    return pl.pallas_call(
        pre_kernel,
        grid=(TOK_DEV // PRE_ROWS,),
        in_specs=[SMEM] * 5 + [rows] * 4 + [gain] * 2,
        out_specs=[pl.BlockSpec((4, PRE_ROWS, LOCAL), lambda i: (0, i, 0))] * WAYS,
        out_shape=[jax.ShapeDtypeStruct((4, TOK_DEV, LOCAL), BF16)] * WAYS,
        scratch_shapes=[pltpu.VMEM((PRE_ROWS, HD), BF16)] * 2,
        compiler_params=params(1),
        cost_estimate=pl.CostEstimate(flops=20_000_000, bytes_accessed=6_300_000, transcendentals=0),
        name="prepare",
    )(dest, res_len, move_len, steps, table, q_in, k_in, v_in, grad_out, q_gain, k_gain)


def nt(a, b):
    return lax.dot_general(a, b, (((1,), (1,)), ((), ())), preferred_element_type=F32)


def tn(a, b):
    return lax.dot_general(a, b, (((0,), (0,)), ((), ())), preferred_element_type=F32)


def grads(q, k, v, g, bias):
    scores = nt(q, k) * SCALE + bias
    top = jnp.max(scores, axis=1, keepdims=True)
    raw = jnp.exp(scores - top)
    weights = raw * (1.0 / jnp.sum(raw, axis=1, keepdims=True))
    attended = jnp.dot(weights.astype(BF16), v, preferred_element_type=F32)
    delta = jnp.sum(g.astype(F32) * attended, axis=1, keepdims=True)
    score_grad = (weights * (nt(g, v) - delta)).astype(BF16)
    query_grad = jnp.dot(score_grad, k, preferred_element_type=F32) * SCALE
    return query_grad, tn(score_grad, q)


QUERY_ROWS = 512
ALL = WAYS * TOK_DEV
ONES = 16
POWER = SCALE * math.log2(math.e)


def flip(block):
    return block.astype(F32).T.astype(BF16)


def attention_kernel(dest_ref, res_ref, move_ref, *rest):
    slots, rest = rest[:WAYS], rest[WAYS:]
    short_ref, qg_ref, kg_ref, out_ref, gain_ref, *rest = rest
    q_ref, k_ref, v_ref, g_ref, qt_ref, kt_ref, vt_ref, gt_ref, dq_ref, dk_ref = rest
    head = pl.program_id(0)
    group = lax.axis_index("dp")
    slot = lax.axis_index("head")
    source = find_source(dest_ref, group)
    stay_len = res_ref[group]
    move_len = move_ref[source]
    peers = [jnp.bitwise_xor(slot, s) for s in range(WAYS)]
    rows = lax.broadcasted_iota(jnp.int32, (TOK_DEV, 1), 0)
    first_lane = lax.broadcasted_iota(jnp.int32, (TOK_DEV, 128), 1) == 0
    for s in range(WAYS):
        here = pl.ds(s * TOK_DEV, TOK_DEV)
        q, k, v = slots[s][0], slots[s][1], slots[s][2]
        g = jnp.where(rows < RES, slots[s][3].astype(F32), 0.0)
        limit = jnp.minimum(stay_len - peers[s] * RES, RES)
        q_ref[here, 0:128] = q
        q_ref[here, 128:256] = jnp.where(first_lane, 1.0, 0.0).astype(BF16)
        k_ref[here, 0:128] = k
        masked = jnp.logical_and(first_lane, rows >= limit)
        k_ref[here, 128:256] = jnp.where(masked, -1e30, 0.0).astype(BF16)
        v_ref[here] = v
        g_ref[here] = g.astype(BF16)
        qt_ref[:, here] = flip(q)
        kt_ref[:, here] = flip(k)
        vt_ref[0:128, here] = flip(v)
        gt_ref[:, here] = g.T
    ones = lax.broadcasted_iota(jnp.int32, (ONES, ALL), 0) == 0
    vt_ref[128 : 128 + ONES, :] = jnp.where(ones, 1.0, 0.0).astype(BF16)

    for i in range(ALL // QUERY_ROWS):
        here = pl.ds(i * QUERY_ROWS, QUERY_ROWS)
        scores = nt(k_ref[...], q_ref[here])
        raw = jnp.exp2((scores - jnp.max(scores, axis=0, keepdims=True)) * POWER)
        attended = jnp.dot(vt_ref[...], raw.astype(BF16), preferred_element_type=F32)
        inverse = 1.0 / attended[128:129]
        delta = jnp.sum(gt_ref[:, here] * attended[0:128], axis=0, keepdims=True) * inverse
        score_grad = (raw * (nt(v_ref[...], g_ref[here]) - delta)).astype(BF16)
        dq = jnp.dot(kt_ref[...], score_grad, preferred_element_type=F32) * (inverse * SCALE)
        dq_ref[here] = dq.T
        dk = nt(score_grad, (qt_ref[:, here].astype(F32) * inverse).astype(BF16))
        if i == 0:
            dk_ref[...] = dk
        else:
            dk_ref[...] += dk

    lines = [short_ref[p].astype(F32) for p in peers]
    short_q = jnp.concatenate([x[0:8] for x in lines], axis=0).astype(BF16)
    short_k = jnp.concatenate([x[8:16] for x in lines], axis=0).astype(BF16)
    short_v = jnp.concatenate([x[16:24] for x in lines], axis=0).astype(BF16)
    short_g = jnp.concatenate(
        [slots[s][3, pl.ds(112, 16)].astype(F32)[8:16] for s in range(WAYS)], axis=0
    ).astype(BF16)
    lane = lax.broadcasted_iota(jnp.int32, (1, WAYS * MOV), 1)
    position = jnp.bitwise_xor(lane // MOV, slot) * MOV + lane % MOV
    short_bias = jnp.where(position < move_len, 0.0, -1e30).astype(F32)
    short_dq, short_dk = grads(short_q, short_k, short_v, short_g, short_bias)
    short_dq = short_dq.astype(BF16).astype(F32)
    short_dk = (short_dk * SCALE).astype(BF16).astype(F32)

    dq = dq_ref[...].astype(BF16)
    dk = (dk_ref[...] * SCALE).astype(BF16)
    for s in range(WAYS):
        for n, stay, short in ((0, dq, short_dq), (1, dk, short_dk)):
            block = stay[s * TOK_DEV : (s + 1) * TOK_DEV].astype(F32)
            block = jnp.concatenate([block[:RES], short[s * MOV : (s + 1) * MOV]], axis=0)
            out_ref[peers[s], n] = block.astype(BF16)

    def total(stay, norm, short, short_norm, gain_ref):
        summed = jnp.sum(stay.astype(F32) * norm.astype(F32), axis=0, keepdims=True)
        summed += jnp.sum(short * short_norm.astype(F32), axis=0, keepdims=True)
        return summed / gain_ref[pl.ds(slot * HEADS + head, 1)]

    gain_ref[pl.ds(head, 1)] = total(dq, q_ref[:, 0:128], short_dq, short_q, qg_ref)
    gain_ref[pl.ds(HEADS + head, 1)] = total(dk, k_ref[:, 0:128], short_dk, short_k, kg_ref)


def attention(dest, res_len, move_len, slots, short, q_gain, k_gain):
    whole = lambda shape: pl.BlockSpec(shape, lambda b: (0,) * len(shape))
    return pl.pallas_call(
        attention_kernel,
        grid=(HEADS,),
        in_specs=[SMEM] * 3
        + [pl.BlockSpec((4, TOK_DEV, 128), lambda b: (0, 0, b))] * WAYS
        + [pl.BlockSpec((WAYS, 32, 128), lambda b: (0, 0, b))]
        + [whole((BLOCKS, 128))] * 2,
        out_specs=[
            pl.BlockSpec((WAYS, 2, TOK_DEV, 128), lambda b: (0, 0, 0, b)),
            whole((8, 128)),
        ],
        out_shape=[
            jax.ShapeDtypeStruct((WAYS, 2, TOK_DEV, LOCAL), BF16),
            jax.ShapeDtypeStruct((8, 128), F32),
        ],
        scratch_shapes=[pltpu.VMEM((ALL, 256), BF16)] * 2
        + [pltpu.VMEM((ALL, 128), BF16)] * 2
        + [pltpu.VMEM((128, ALL), BF16)] * 2
        + [pltpu.VMEM((128 + ONES, ALL), BF16), pltpu.VMEM((128, ALL), F32)]
        + [pltpu.VMEM((ALL, 128), F32)] * 2,
        compiler_params=params(1),
        cost_estimate=pl.CostEstimate(
            flops=4_000_000_000, bytes_accessed=5_000_000, transcendentals=3_200_000
        ),
        name="attention",
    )(dest, res_len, move_len, *slots, short, q_gain, k_gain)


POST_ROWS = 32


def post_kernel(q_ref, k_ref, raw_ref, qg_ref, kg_ref, dq_ref, dk_ref, oq_ref, ok_ref):
    last = pl.program_id(0) == TOK_DEV // POST_ROWS - 1
    row = lax.broadcasted_iota(jnp.int32, (POST_ROWS, 1), 0)
    use_short = jnp.logical_and(last, row >= POST_ROWS - MOV)

    def one(in_ref, which, gain_ref, grad_ref, out_ref):
        short = raw_ref[which].astype(F32)
        short = jnp.concatenate([jnp.zeros((POST_ROWS - 16, HD), F32), short], axis=0)
        x = jnp.where(use_short, short, in_ref[...].astype(F32))
        scale = lax.rsqrt(jnp.sum(x * x, axis=1, keepdims=True) / HD + EPS)
        gain = gain_ref[...]
        grad = jnp.concatenate([grad_ref[p, 0].astype(F32) for p in range(WAYS)], axis=1) * gain
        dots = jnp.sum(x * grad, axis=1, keepdims=True)
        out_ref[...] = (scale * grad - x * ((scale * scale * scale) * dots / HD)).astype(BF16)

    one(q_ref, 0, qg_ref, dq_ref, oq_ref)
    one(k_ref, 1, kg_ref, dk_ref, ok_ref)


def finish(q_in, k_in, raw, q_gain, k_gain, back):
    rows = pl.BlockSpec((POST_ROWS, HD), lambda i: (i, 0))
    gain = pl.BlockSpec((1, HD), lambda i: (0, 0))
    return pl.pallas_call(
        post_kernel,
        grid=(TOK_DEV // POST_ROWS,),
        in_specs=[
            rows,
            rows,
            pl.BlockSpec((2, 16, HD), lambda i: (0, 0, 0)),
            gain,
            gain,
            pl.BlockSpec((WAYS, 1, POST_ROWS, LOCAL), lambda i: (0, 0, i, 0)),
            pl.BlockSpec((WAYS, 1, POST_ROWS, LOCAL), lambda i: (0, 1, i, 0)),
        ],
        out_specs=[rows, rows],
        out_shape=[jax.ShapeDtypeStruct((TOK_DEV, HD), BF16)] * 2,
        compiler_params=params(1),
        cost_estimate=pl.CostEstimate(flops=20_000_000, bytes_accessed=4_800_000, transcendentals=0),
        name="finish",
    )(q_in, k_in, raw, q_gain, k_gain, back, back)


AHEAD = 4


def swap_all(x, axis):
    return lax.all_to_all(x, axis, split_axis=0, concat_axis=0, tiled=True)


def gather_sum(x, rings):
    return jnp.sum(lax.all_gather(x, "dp", axis_index_groups=rings), axis=0)


def local(
    q_in, k_in, v_in, grad_out, q_gain, k_gain,
    res_len, move_len, step_index, dest_group, loss_weight,
):
    gain_q, gain_k = q_gain.reshape(1, HD), k_gain.reshape(1, HD)
    packed, grad_rows = lax.optimization_barrier((pack_short(q_in, k_in, v_in), grad_out))
    spread = swap_all(packed, "dp")
    own, *outgoing = prepare(
        dest_group, res_len, move_len, step_index, loss_weight,
        q_in, k_in, v_in, grad_rows, gain_q, gain_k,
    )
    arrived = [own] + [
        lax.ppermute(x, "head", [(i, i ^ (n + 1)) for i in range(WAYS)])
        for n, x in enumerate(outgoing)
    ]
    held = lax.optimization_barrier((spread, *arrived[1 : 1 + AHEAD]))
    spread, arrived[1 : 1 + AHEAD] = held[0], held[1:]
    routed = swap_all(scatter_short(dest_group, spread), "dp")
    short, raw = unpack_short(routed, gain_q, gain_k)
    short = swap_all(short, "head")
    grad, part = attention(
        dest_group, res_len, move_len, arrived, short,
        q_gain.reshape(BLOCKS, 128), k_gain.reshape(BLOCKS, 128),
    )
    back = swap_all(grad, "head")
    total = gather_sum(gather_sum(part, ZRING), PLANE)
    out_q, out_k = finish(q_in, k_in, raw, gain_q, gain_k, back)
    return (
        out_q,
        out_k,
        total[:HEADS].reshape(LOCAL),
        total[HEADS : 2 * HEADS].reshape(LOCAL),
    )


def solution(mesh):
    tokens = P(("dp", "head"), None)
    return jax.shard_map(
        local,
        mesh=mesh,
        in_specs=(tokens,) * 4 + (P(),) * 7,
        out_specs=(tokens, tokens, P("head"), P("head")),
        check_vma=False,
    )
```

```python
import math

import jax
import jax.numpy as jnp
from jax import lax
from jax.experimental import pallas as pl
from jax.experimental.pallas import tpu as pltpu
from jax.sharding import PartitionSpec as P

HEAD_DIM = 128
TOK_DEV = 128
MOV = 8
RES = 120
EPS = 1e-06
WAYS = 8
GROUPS = 64
HD = 3072
LOCAL = HD // WAYS
HEADS = LOCAL // HEAD_DIM
BLOCKS = HD // 128
SCALE = 1.0 / math.sqrt(HEAD_DIM)
F32 = jnp.float32
BF16 = jnp.bfloat16
VMEM_LIMIT = 56 * 1024 * 1024

PLANE = [[xl * 32 + z * 2 + c for xl in range(2) for c in range(2)] for z in range(16)]
ZRING = [[xl * 32 + z * 2 + c for z in range(16)] for xl in range(2) for c in range(2)]

SMEM = pl.BlockSpec(memory_space=pltpu.SMEM)


def params(count=0):
    return pltpu.CompilerParams(
        vmem_limit_bytes=VMEM_LIMIT,
        dimension_semantics=("arbitrary",) * count if count else None,
    )


def find_source(dest_ref, group):
    return lax.fori_loop(
        0, GROUPS, lambda g, found: jnp.where(dest_ref[g] == group, g, found), jnp.int32(0)
    )


def pack_kernel(q_ref, k_ref, v_ref, out_ref):
    q = q_ref[...].astype(F32)[8:16]
    k = k_ref[...].astype(F32)[8:16]
    v = v_ref[...].astype(F32)[8:16]
    pair = jnp.concatenate([q, k], axis=0).astype(BF16)
    half = HD // 2
    tail = jnp.concatenate([v[:, :half], v[:, half:]], axis=0).astype(BF16)
    for c in range(BLOCKS):
        out_ref[c] = pair[:, c * 128 : (c + 1) * 128]
    for c in range(BLOCKS // 2):
        out_ref[BLOCKS + c] = tail[:, c * 128 : (c + 1) * 128]
    rest = GROUPS - BLOCKS - BLOCKS // 2
    out_ref[pl.ds(BLOCKS + BLOCKS // 2, rest)] = jnp.zeros((rest, 16, 128), BF16)


def pack_short(q_in, k_in, v_in):
    spec = pl.BlockSpec((16, HD), lambda i: (TOK_DEV // 16 - 1, 0))
    return pl.pallas_call(
        pack_kernel,
        grid=(1,),
        in_specs=[spec] * 3,
        out_specs=pl.BlockSpec((GROUPS, 16, 128), lambda i: (0, 0, 0)),
        out_shape=jax.ShapeDtypeStruct((GROUPS, 16, 128), BF16),
        compiler_params=params(1),
        name="pack_short",
    )(q_in, k_in, v_in)


def scatter_kernel(dest_ref, in_ref, out_ref):
    def step(g, carry):
        out_ref[dest_ref[g]] = in_ref[g]
        return carry

    lax.fori_loop(0, GROUPS, step, 0)


def scatter_short(dest_group, parts):
    whole = pl.BlockSpec(memory_space=pltpu.VMEM)
    return pl.pallas_call(
        scatter_kernel,
        in_specs=[SMEM, whole],
        out_specs=whole,
        out_shape=jax.ShapeDtypeStruct(parts.shape, BF16),
        compiler_params=params(),
        name="scatter_short",
    )(dest_group, parts)


def norm_rows(rows, gain):
    scale = lax.rsqrt(jnp.sum(rows * rows, axis=1, keepdims=True) / HD + EPS)
    return rows * scale * gain


def unpack_kernel(in_ref, qg_ref, kg_ref, send_ref, raw_ref):
    pair = jnp.concatenate([in_ref[c] for c in range(BLOCKS)], axis=1).astype(F32)
    tail = jnp.concatenate([in_ref[BLOCKS + c] for c in range(BLOCKS // 2)], axis=1).astype(F32)
    q, k = pair[0:8], pair[8:16]
    v = jnp.concatenate([tail[0:8], tail[8:16]], axis=1)
    qn = norm_rows(q, qg_ref[...])
    kn = norm_rows(k, kg_ref[...])
    zero = jnp.zeros((8, HD), F32)
    first = jnp.concatenate([qn, kn], axis=0).astype(BF16)
    second = jnp.concatenate([v, zero], axis=0).astype(BF16)
    for p in range(WAYS):
        send_ref[p, 0:16, :] = first[:, p * LOCAL : (p + 1) * LOCAL]
        send_ref[p, 16:32, :] = second[:, p * LOCAL : (p + 1) * LOCAL]
    raw_ref[0] = jnp.concatenate([zero, q], axis=0).astype(BF16)
    raw_ref[1] = jnp.concatenate([zero, k], axis=0).astype(BF16)


def unpack_short(parts, q_gain, k_gain):
    whole = pl.BlockSpec(memory_space=pltpu.VMEM)
    return pl.pallas_call(
        unpack_kernel,
        in_specs=[whole] * 3,
        out_specs=[whole] * 2,
        out_shape=[
            jax.ShapeDtypeStruct((WAYS, 32, LOCAL), BF16),
            jax.ShapeDtypeStruct((2, 16, HD), BF16),
        ],
        compiler_params=params(),
        name="unpack_short",
    )(parts, q_gain, k_gain)


PRE_ROWS = 32


def split_kernel(dest_ref, res_ref, move_ref, step_ref, table_ref, v_ref, go_ref, *outs):
    group = lax.axis_index("dp")
    slot = lax.axis_index("head")
    source = find_source(dest_ref, group)
    stay_weight = table_ref[step_ref[group, 0]]
    move_weight = table_ref[step_ref[source, 1]]
    rows = pl.program_id(0) * PRE_ROWS + lax.broadcasted_iota(jnp.int32, (PRE_ROWS, 1), 0)
    stay = jnp.where(slot * RES + rows < res_ref[group], stay_weight, 0.0)
    move = jnp.where(slot * MOV + rows - RES < move_ref[source], move_weight, 0.0)
    weight = jnp.where(rows < RES, stay, move)
    for s in range(WAYS):
        start = pl.multiple_of(jnp.bitwise_xor(slot, s) * LOCAL, 128)
        cols = pl.ds(start, LOCAL)
        outs[s][0] = v_ref[:, cols]
        outs[s][1] = (go_ref[:, cols].astype(F32) * weight).astype(BF16)


def split_rows(dest, res_len, move_len, steps, table, v_in, grad_out):
    rows = pl.BlockSpec((PRE_ROWS, HD), lambda i: (i, 0))
    return pl.pallas_call(
        split_kernel,
        grid=(TOK_DEV // PRE_ROWS,),
        in_specs=[SMEM] * 5 + [rows] * 2,
        out_specs=[pl.BlockSpec((2, PRE_ROWS, LOCAL), lambda i: (0, i, 0))] * WAYS,
        out_shape=[jax.ShapeDtypeStruct((2, TOK_DEV, LOCAL), BF16)] * WAYS,
        compiler_params=params(1),
        cost_estimate=pl.CostEstimate(flops=1_000_000, bytes_accessed=3_200_000, transcendentals=0),
        name="split_rows",
    )(dest, res_len, move_len, steps, table, v_in, grad_out)


def norm_kernel(q_ref, k_ref, qg_ref, kg_ref, out_ref):
    for n, (in_ref, gain_ref) in enumerate(((q_ref, qg_ref), (k_ref, kg_ref))):
        normed = norm_rows(in_ref[...].astype(F32), gain_ref[...]).astype(BF16)
        for p in range(WAYS):
            out_ref[p, n] = normed[:, p * LOCAL : (p + 1) * LOCAL]


def norm_split(q_in, k_in, q_gain, k_gain):
    rows = pl.BlockSpec((PRE_ROWS, HD), lambda i: (i, 0))
    gain = pl.BlockSpec((1, HD), lambda i: (0, 0))
    return pl.pallas_call(
        norm_kernel,
        grid=(TOK_DEV // PRE_ROWS,),
        in_specs=[rows] * 2 + [gain] * 2,
        out_specs=pl.BlockSpec((WAYS, 2, PRE_ROWS, LOCAL), lambda i: (0, 0, i, 0)),
        out_shape=jax.ShapeDtypeStruct((WAYS, 2, TOK_DEV, LOCAL), BF16),
        compiler_params=params(1),
        cost_estimate=pl.CostEstimate(flops=5_000_000, bytes_accessed=3_200_000, transcendentals=0),
        name="norm_split",
    )(q_in, k_in, q_gain, k_gain)


def nt(a, b):
    return lax.dot_general(a, b, (((1,), (1,)), ((), ())), preferred_element_type=F32)


def tn(a, b):
    return lax.dot_general(a, b, (((0,), (0,)), ((), ())), preferred_element_type=F32)


def grads(q, k, v, g, bias):
    scores = nt(q, k) * SCALE + bias
    top = jnp.max(scores, axis=1, keepdims=True)
    raw = jnp.exp(scores - top)
    weights = raw * (1.0 / jnp.sum(raw, axis=1, keepdims=True))
    attended = jnp.dot(weights.astype(BF16), v, preferred_element_type=F32)
    delta = jnp.sum(g.astype(F32) * attended, axis=1, keepdims=True)
    score_grad = (weights * (nt(g, v) - delta)).astype(BF16)
    query_grad = jnp.dot(score_grad, k, preferred_element_type=F32) * SCALE
    return query_grad, tn(score_grad, q)


QUERY_ROWS = 512
ALL = WAYS * TOK_DEV
ONES = 16
POWER = SCALE * math.log2(math.e)


def flip(block):
    return block.astype(F32).T.astype(BF16)


def attention_kernel(res_ref, qk_ref, *rest):
    slots, rest = rest[:WAYS], rest[WAYS:]
    qg_ref, kg_ref, out_ref, gain_ref, *rest = rest
    q_ref, k_ref, v_ref, g_ref, qt_ref, kt_ref, vt_ref, gt_ref, dq_ref, dk_ref = rest
    head = pl.program_id(0)
    slot = lax.axis_index("head")
    stay_len = res_ref[lax.axis_index("dp")]
    peers = [jnp.bitwise_xor(slot, s) for s in range(WAYS)]
    rows = lax.broadcasted_iota(jnp.int32, (TOK_DEV, 1), 0)
    first_lane = lax.broadcasted_iota(jnp.int32, (TOK_DEV, 128), 1) == 0
    for s in range(WAYS):
        here = pl.ds(s * TOK_DEV, TOK_DEV)
        q, k, v = qk_ref[peers[s], 0], qk_ref[peers[s], 1], slots[s][0]
        g = jnp.where(rows < RES, slots[s][1].astype(F32), 0.0)
        limit = jnp.minimum(stay_len - peers[s] * RES, RES)
        q_ref[here, 0:128] = q
        q_ref[here, 128:256] = jnp.where(first_lane, 1.0, 0.0).astype(BF16)
        k_ref[here, 0:128] = k
        masked = jnp.logical_and(first_lane, rows >= limit)
        k_ref[here, 128:256] = jnp.where(masked, -1e30, 0.0).astype(BF16)
        v_ref[here] = v
        g_ref[here] = g.astype(BF16)
        qt_ref[:, here] = flip(q)
        kt_ref[:, here] = flip(k)
        vt_ref[0:128, here] = flip(v)
        gt_ref[:, here] = g.T
    ones = lax.broadcasted_iota(jnp.int32, (ONES, ALL), 0) == 0
    vt_ref[128 : 128 + ONES, :] = jnp.where(ones, 1.0, 0.0).astype(BF16)

    for i in range(ALL // QUERY_ROWS):
        here = pl.ds(i * QUERY_ROWS, QUERY_ROWS)
        scores = nt(k_ref[...], q_ref[here])
        raw = jnp.exp2((scores - jnp.max(scores, axis=0, keepdims=True)) * POWER)
        attended = jnp.dot(vt_ref[...], raw.astype(BF16), preferred_element_type=F32)
        inverse = 1.0 / attended[128:129]
        delta = jnp.sum(gt_ref[:, here] * attended[0:128], axis=0, keepdims=True) * inverse
        score_grad = (raw * (nt(v_ref[...], g_ref[here]) - delta)).astype(BF16)
        dq = jnp.dot(kt_ref[...], score_grad, preferred_element_type=F32) * (inverse * SCALE)
        dq_ref[here] = dq.T
        dk = nt(score_grad, (qt_ref[:, here].astype(F32) * inverse).astype(BF16))
        if i == 0:
            dk_ref[...] = dk
        else:
            dk_ref[...] += dk

    dq = dq_ref[...].astype(BF16)
    dk = (dk_ref[...] * SCALE).astype(BF16)
    for s in range(WAYS):
        out_ref[peers[s], 0] = dq[s * TOK_DEV : (s + 1) * TOK_DEV]
        out_ref[peers[s], 1] = dk[s * TOK_DEV : (s + 1) * TOK_DEV]

    def total(grad, norm, gain_ref):
        summed = jnp.sum(grad.astype(F32) * norm.astype(F32), axis=0, keepdims=True)
        return summed / gain_ref[pl.ds(slot * HEADS + head, 1)]

    gain_ref[pl.ds(head, 1)] = total(dq, q_ref[:, 0:128], qg_ref)
    gain_ref[pl.ds(HEADS + head, 1)] = total(dk, k_ref[:, 0:128], kg_ref)


def whole_block(shape):
    return pl.BlockSpec(shape, lambda b: (0,) * len(shape))


def attention(res_len, spread, slots, q_gain, k_gain):
    heads = pl.BlockSpec((WAYS, 2, TOK_DEV, 128), lambda b: (0, 0, 0, b))
    return pl.pallas_call(
        attention_kernel,
        grid=(HEADS,),
        in_specs=[SMEM, heads]
        + [pl.BlockSpec((2, TOK_DEV, 128), lambda b: (0, 0, b))] * WAYS
        + [whole_block((BLOCKS, 128))] * 2,
        out_specs=[heads, whole_block((8, 128))],
        out_shape=[
            jax.ShapeDtypeStruct((WAYS, 2, TOK_DEV, LOCAL), BF16),
            jax.ShapeDtypeStruct((8, 128), F32),
        ],
        scratch_shapes=[pltpu.VMEM((ALL, 256), BF16)] * 2
        + [pltpu.VMEM((ALL, 128), BF16)] * 2
        + [pltpu.VMEM((128, ALL), BF16)] * 2
        + [pltpu.VMEM((128 + ONES, ALL), BF16), pltpu.VMEM((128, ALL), F32)]
        + [pltpu.VMEM((ALL, 128), F32)] * 2,
        compiler_params=params(1),
        cost_estimate=pl.CostEstimate(
            flops=4_000_000_000, bytes_accessed=5_000_000, transcendentals=3_200_000
        ),
        name="attention",
    )(res_len, spread, *slots, q_gain, k_gain)


def short_kernel(dest_ref, move_ref, short_ref, *rest):
    slots, rest = rest[:WAYS], rest[WAYS:]
    grad_ref, part_ref, qg_ref, kg_ref, out_ref, gain_ref = rest
    head = pl.program_id(0)
    slot = lax.axis_index("head")
    move_len = move_ref[find_source(dest_ref, lax.axis_index("dp"))]
    peers = [jnp.bitwise_xor(slot, s) for s in range(WAYS)]
    lines = [short_ref[p].astype(F32) for p in peers]
    q = jnp.concatenate([x[0:8] for x in lines], axis=0).astype(BF16)
    k = jnp.concatenate([x[8:16] for x in lines], axis=0).astype(BF16)
    v = jnp.concatenate([x[16:24] for x in lines], axis=0).astype(BF16)
    g = jnp.concatenate([x[0].astype(F32)[8:16] for x in slots], axis=0).astype(BF16)
    lane = lax.broadcasted_iota(jnp.int32, (1, WAYS * MOV), 1)
    position = jnp.bitwise_xor(lane // MOV, slot) * MOV + lane % MOV
    bias = jnp.where(position < move_len, 0.0, -1e30).astype(F32)
    dq, dk = grads(q, k, v, g, bias)
    dq = dq.astype(BF16).astype(F32)
    dk = (dk * SCALE).astype(BF16).astype(F32)
    for s in range(WAYS):
        for n, grad in ((0, dq), (1, dk)):
            kept = grad_ref[peers[s], n].astype(F32)[0:8]
            block = jnp.concatenate([kept, grad[s * MOV : (s + 1) * MOV]], axis=0)
            out_ref[peers[s], n] = block.astype(BF16)

    @pl.when(head == 0)
    def _():
        gain_ref[...] = part_ref[...]

    def total(grad, norm, gain_ref):
        summed = jnp.sum(grad * norm.astype(F32), axis=0, keepdims=True)
        return summed / gain_ref[pl.ds(slot * HEADS + head, 1)]

    gain_ref[pl.ds(head, 1)] += total(dq, q, qg_ref)
    gain_ref[pl.ds(HEADS + head, 1)] += total(dk, k, kg_ref)


def short_attention(dest, move_len, short, slots, grad, part, q_gain, k_gain):
    tail = TOK_DEV // 16 - 1
    rows = pl.BlockSpec((WAYS, 2, 16, 128), lambda b: (0, 0, tail, b))
    return pl.pallas_call(
        short_kernel,
        grid=(HEADS,),
        in_specs=[SMEM] * 2
        + [pl.BlockSpec((WAYS, 32, 128), lambda b: (0, 0, b))]
        + [pl.BlockSpec((1, 16, 128), lambda b: (1, tail, b))] * WAYS
        + [rows]
        + [whole_block((8, 128))]
        + [whole_block((BLOCKS, 128))] * 2,
        out_specs=[rows, whole_block((8, 128))],
        out_shape=[
            jax.ShapeDtypeStruct(grad.shape, BF16),
            jax.ShapeDtypeStruct((8, 128), F32),
        ],
        input_output_aliases={3 + WAYS: 0},
        compiler_params=params(1),
        cost_estimate=pl.CostEstimate(
            flops=20_000_000, bytes_accessed=1_000_000, transcendentals=12_000
        ),
        name="short_attention",
    )(dest, move_len, short, *slots, grad, part, q_gain, k_gain)


POST_ROWS = 32


def post_kernel(q_ref, k_ref, raw_ref, qg_ref, kg_ref, dq_ref, dk_ref, oq_ref, ok_ref):
    last = pl.program_id(0) == TOK_DEV // POST_ROWS - 1
    row = lax.broadcasted_iota(jnp.int32, (POST_ROWS, 1), 0)
    use_short = jnp.logical_and(last, row >= POST_ROWS - MOV)

    def one(in_ref, which, gain_ref, grad_ref, out_ref):
        short = raw_ref[which].astype(F32)
        short = jnp.concatenate([jnp.zeros((POST_ROWS - 16, HD), F32), short], axis=0)
        x = jnp.where(use_short, short, in_ref[...].astype(F32))
        scale = lax.rsqrt(jnp.sum(x * x, axis=1, keepdims=True) / HD + EPS)
        gain = gain_ref[...]
        grad = jnp.concatenate([grad_ref[p, 0].astype(F32) for p in range(WAYS)], axis=1) * gain
        dots = jnp.sum(x * grad, axis=1, keepdims=True)
        out_ref[...] = (scale * grad - x * ((scale * scale * scale) * dots / HD)).astype(BF16)

    one(q_ref, 0, qg_ref, dq_ref, oq_ref)
    one(k_ref, 1, kg_ref, dk_ref, ok_ref)


def finish(q_in, k_in, raw, q_gain, k_gain, back):
    rows = pl.BlockSpec((POST_ROWS, HD), lambda i: (i, 0))
    gain = pl.BlockSpec((1, HD), lambda i: (0, 0))
    return pl.pallas_call(
        post_kernel,
        grid=(TOK_DEV // POST_ROWS,),
        in_specs=[
            rows,
            rows,
            pl.BlockSpec((2, 16, HD), lambda i: (0, 0, 0)),
            gain,
            gain,
            pl.BlockSpec((WAYS, 1, POST_ROWS, LOCAL), lambda i: (0, 0, i, 0)),
            pl.BlockSpec((WAYS, 1, POST_ROWS, LOCAL), lambda i: (0, 1, i, 0)),
        ],
        out_specs=[rows, rows],
        out_shape=[jax.ShapeDtypeStruct((TOK_DEV, HD), BF16)] * 2,
        compiler_params=params(1),
        cost_estimate=pl.CostEstimate(flops=20_000_000, bytes_accessed=4_800_000, transcendentals=0),
        name="finish",
    )(q_in, k_in, raw, q_gain, k_gain, back, back)


AHEAD = 4


def swap_all(x, axis):
    return lax.all_to_all(x, axis, split_axis=0, concat_axis=0, tiled=True)


def gather_sum(x, rings):
    return jnp.sum(lax.all_gather(x, "dp", axis_index_groups=rings), axis=0)


def local(
    q_in, k_in, v_in, grad_out, q_gain, k_gain,
    res_len, move_len, step_index, dest_group, loss_weight,
):
    gain_q, gain_k = q_gain.reshape(1, HD), k_gain.reshape(1, HD)
    own, *outgoing = split_rows(
        dest_group, res_len, move_len, step_index, loss_weight, v_in, grad_out
    )
    outgoing, v_rows = lax.optimization_barrier((outgoing, v_in))
    spread = swap_all(pack_short(q_in, k_in, v_rows), "dp")
    slots = [own] + [
        lax.ppermute(x, "head", [(i, i ^ (n + 1)) for i in range(WAYS)])
        for n, x in enumerate(outgoing)
    ]
    normed = norm_split(q_in, k_in, gain_q, gain_k)
    spread, normed, slots[1 : 1 + AHEAD] = lax.optimization_barrier(
        (spread, normed, slots[1 : 1 + AHEAD])
    )
    placed = scatter_short(dest_group, spread)
    blocks = swap_all(normed, "head")
    placed, blocks, slots[1 + AHEAD :] = lax.optimization_barrier(
        (placed, blocks, slots[1 + AHEAD :])
    )
    routed = swap_all(placed, "dp")
    gain_q_rows, gain_k_rows = q_gain.reshape(BLOCKS, 128), k_gain.reshape(BLOCKS, 128)
    grad, part = attention(res_len, blocks, slots, gain_q_rows, gain_k_rows)
    routed, part = lax.optimization_barrier((routed, part))
    short, raw = unpack_short(routed, gain_q, gain_k)
    short = swap_all(short, "head")
    grad, part = short_attention(
        dest_group, move_len, short, slots, grad, part, gain_q_rows, gain_k_rows
    )
    back = swap_all(grad, "head")
    total = gather_sum(gather_sum(part, ZRING), PLANE)
    out_q, out_k = finish(q_in, k_in, raw, gain_q, gain_k, back)
    return (
        out_q,
        out_k,
        total[:HEADS].reshape(LOCAL),
        total[HEADS : 2 * HEADS].reshape(LOCAL),
    )


def solution(mesh):
    tokens = P(("dp", "head"), None)
    return jax.shard_map(
        local,
        mesh=mesh,
        in_specs=(tokens,) * 4 + (P(),) * 7,
        out_specs=(tokens, tokens, P("head"), P("head")),
        check_vma=False,
    )
```

```python
import math

import jax
import jax.numpy as jnp
from jax import lax
from jax.experimental import pallas as pl
from jax.experimental.pallas import tpu as pltpu
from jax.sharding import PartitionSpec as P

HEAD_DIM = 128
TOK_DEV = 128
MOV = 8
RES = 120
EPS = 1e-06
WAYS = 8
GROUPS = 64
HD = 3072
LOCAL = HD // WAYS
HEADS = LOCAL // HEAD_DIM
BLOCKS = HD // 128
SCALE = 1.0 / math.sqrt(HEAD_DIM)
F32 = jnp.float32
BF16 = jnp.bfloat16
VMEM_LIMIT = 56 * 1024 * 1024

PLANE = [[xl * 32 + z * 2 + c for xl in range(2) for c in range(2)] for z in range(16)]
ZRING = [[xl * 32 + z * 2 + c for z in range(16)] for xl in range(2) for c in range(2)]

SMEM = pl.BlockSpec(memory_space=pltpu.SMEM)


def params(count=0):
    return pltpu.CompilerParams(
        vmem_limit_bytes=VMEM_LIMIT,
        dimension_semantics=("arbitrary",) * count if count else None,
    )


def find_source(dest_ref, group):
    return lax.fori_loop(
        0, GROUPS, lambda g, found: jnp.where(dest_ref[g] == group, g, found), jnp.int32(0)
    )


TAIL = TOK_DEV - 16
EXTRA = 4 * TOK_DEV
SENT = EXTRA + 16
PAIRS = WAYS // 2
SCALES = 3 * HEADS * PAIRS


def pack_kernel(q_ref, k_ref, v_ref, scale_ref, out_ref):
    def pair(ref, i, first):
        rows = [ref[j].astype(F32)[first : first + 8] for j in (2 * i, 2 * i + 1)]
        return jnp.concatenate(rows, axis=0).astype(BF16)

    for i in range(PAIRS):
        for n, ref in enumerate((q_ref, k_ref, v_ref)):
            rows = pair(ref, i, 8)
            for b in range(HEADS):
                out_ref[(n * HEADS + b) * PAIRS + i] = rows[:, b * 128 : (b + 1) * 128]
        out_ref[SCALES + i] = pair(scale_ref, i, 0)
    rest = GROUPS - SCALES - PAIRS
    out_ref[pl.ds(SCALES + PAIRS, rest)] = jnp.zeros((rest, 16, 128), BF16)


def pack_short(blocks):
    def rows(n, width):
        return pl.BlockSpec((WAYS, 16, width), lambda i: (0, n, 0))

    return pl.pallas_call(
        pack_kernel,
        grid=(1,),
        in_specs=[rows((n * TOK_DEV + TAIL) // 16, LOCAL) for n in range(3)]
        + [rows(EXTRA // 16, 128)],
        out_specs=pl.BlockSpec((GROUPS, 16, 128), lambda i: (0, 0, 0)),
        out_shape=jax.ShapeDtypeStruct((GROUPS, 16, 128), BF16),
        compiler_params=params(1),
        name="pack_short",
    )(blocks, blocks, blocks, blocks)


def scatter_kernel(dest_ref, in_ref, out_ref):
    def step(g, carry):
        out_ref[dest_ref[g]] = in_ref[g]
        return carry

    lax.fori_loop(0, GROUPS, step, 0)


def scatter_short(dest_group, parts):
    whole = pl.BlockSpec(memory_space=pltpu.VMEM)
    return pl.pallas_call(
        scatter_kernel,
        in_specs=[SMEM, whole],
        out_specs=whole,
        out_shape=jax.ShapeDtypeStruct(parts.shape, BF16),
        compiler_params=params(),
        name="scatter_short",
    )(dest_group, parts)


PRE_ROWS = 32


def row_scale(rows):
    return lax.rsqrt(jnp.sum(rows * rows, axis=1, keepdims=True) / HD + EPS)


def two_terms(scale):
    high = scale.astype(BF16).astype(F32)
    return high, scale - high


def pre_kernel(
    dest_ref, res_ref, move_ref, step_ref, table_ref,
    q_ref, k_ref, v_ref, go_ref, qg_ref, kg_ref, out_ref,
):
    step = pl.program_id(0)
    group = lax.axis_index("dp")
    slot = lax.axis_index("head")
    source = find_source(dest_ref, group)
    stay_weight = table_ref[step_ref[group, 0]]
    move_weight = table_ref[step_ref[source, 1]]
    rows = step * PRE_ROWS + lax.broadcasted_iota(jnp.int32, (PRE_ROWS, 1), 0)
    stay = jnp.where(slot * RES + rows < res_ref[group], stay_weight, 0.0)
    move = jnp.where(slot * MOV + rows - RES < move_ref[source], move_weight, 0.0)
    weight = jnp.where(rows < RES, stay, move)
    start = pl.multiple_of(step * PRE_ROWS, PRE_ROWS)

    def put(n, values):
        for p in range(WAYS):
            out_ref[p, pl.ds(n * TOK_DEV + start, PRE_ROWS), :] = values[
                :, p * LOCAL : (p + 1) * LOCAL
            ]

    terms = []
    for n, (in_ref, gain_ref) in enumerate(((q_ref, qg_ref), (k_ref, kg_ref))):
        x = in_ref[...].astype(F32)
        scale = row_scale(x)
        put(n, (x * scale * gain_ref[...]).astype(BF16))
        terms += two_terms(scale[PRE_ROWS - MOV :])
    put(2, v_ref[...])
    put(3, (go_ref[...].astype(F32) * weight).astype(BF16))

    @pl.when(step == TOK_DEV // PRE_ROWS - 1)
    def _():
        lane = lax.broadcasted_iota(jnp.int32, (MOV, LOCAL), 1)
        scales = jnp.zeros((MOV, LOCAL), F32)
        for n, term in enumerate(terms):
            scales = jnp.where(lane == n, term, scales)
        scales = jnp.concatenate([scales, jnp.zeros((16 - MOV, LOCAL), F32)], axis=0)
        for p in range(WAYS):
            out_ref[p, EXTRA:SENT, :] = scales.astype(BF16)


def prepare(dest, res_len, move_len, steps, table, q_in, k_in, v_in, grad_out, q_gain, k_gain):
    rows = pl.BlockSpec((PRE_ROWS, HD), lambda i: (i, 0))
    gain = pl.BlockSpec((1, HD), lambda i: (0, 0))
    return pl.pallas_call(
        pre_kernel,
        grid=(TOK_DEV // PRE_ROWS,),
        in_specs=[SMEM] * 5 + [rows] * 4 + [gain] * 2,
        out_specs=pl.BlockSpec((WAYS, SENT, LOCAL), lambda i: (0, 0, 0)),
        out_shape=jax.ShapeDtypeStruct((WAYS, SENT, LOCAL), BF16),
        compiler_params=params(1),
        cost_estimate=pl.CostEstimate(flops=20_000_000, bytes_accessed=6_300_000, transcendentals=0),
        name="prepare",
    )(dest, res_len, move_len, steps, table, q_in, k_in, v_in, grad_out, q_gain, k_gain)


def nt(a, b):
    return lax.dot_general(a, b, (((1,), (1,)), ((), ())), preferred_element_type=F32)


def tn(a, b):
    return lax.dot_general(a, b, (((0,), (0,)), ((), ())), preferred_element_type=F32)


def grads(q, k, v, g, bias):
    scores = nt(q, k) * SCALE + bias
    top = jnp.max(scores, axis=1, keepdims=True)
    raw = jnp.exp(scores - top)
    weights = raw * (1.0 / jnp.sum(raw, axis=1, keepdims=True))
    attended = jnp.dot(weights.astype(BF16), v, preferred_element_type=F32)
    delta = jnp.sum(g.astype(F32) * attended, axis=1, keepdims=True)
    score_grad = (weights * (nt(g, v) - delta)).astype(BF16)
    query_grad = jnp.dot(score_grad, k, preferred_element_type=F32) * SCALE
    return query_grad, tn(score_grad, q)


QUERY_ROWS = 512
ALL = WAYS * TOK_DEV
ONES = 16
POWER = SCALE * math.log2(math.e)


def flip(block):
    return block.astype(F32).T.astype(BF16)


BACK_MORE = 32
BACK_HEAD = 64
BACK = BACK_HEAD + 2 * TAIL


def attention_kernel(res_ref, in_ref, qg_ref, kg_ref, out_ref, gain_ref, *rest):
    q_ref, k_ref, v_ref, g_ref, qt_ref, kt_ref, vt_ref, gt_ref, dq_ref, dk_ref = rest
    head = pl.program_id(0)
    slot = lax.axis_index("head")
    stay_len = res_ref[lax.axis_index("dp")]
    rows = lax.broadcasted_iota(jnp.int32, (TOK_DEV, 1), 0)
    first_lane = lax.broadcasted_iota(jnp.int32, (TOK_DEV, 128), 1) == 0
    for s in range(WAYS):
        here = pl.ds(s * TOK_DEV, TOK_DEV)
        q, k, v, g = (in_ref[s, n * TOK_DEV : (n + 1) * TOK_DEV] for n in range(4))
        g = jnp.where(rows < RES, g.astype(F32), 0.0)
        limit = jnp.minimum(stay_len - s * RES, RES)
        q_ref[here, 0:128] = q
        q_ref[here, 128:256] = jnp.where(first_lane, 1.0, 0.0).astype(BF16)
        k_ref[here, 0:128] = k
        masked = jnp.logical_and(first_lane, rows >= limit)
        k_ref[here, 128:256] = jnp.where(masked, -1e30, 0.0).astype(BF16)
        v_ref[here] = v
        g_ref[here] = g.astype(BF16)
        qt_ref[:, here] = flip(q)
        kt_ref[:, here] = flip(k)
        vt_ref[0:128, here] = flip(v)
        gt_ref[:, here] = g.T
    ones = lax.broadcasted_iota(jnp.int32, (ONES, ALL), 0) == 0
    vt_ref[128 : 128 + ONES, :] = jnp.where(ones, 1.0, 0.0).astype(BF16)

    for i in range(ALL // QUERY_ROWS):
        here = pl.ds(i * QUERY_ROWS, QUERY_ROWS)
        scores = nt(k_ref[...], q_ref[here])
        raw = jnp.exp2((scores - jnp.max(scores, axis=0, keepdims=True)) * POWER)
        attended = jnp.dot(vt_ref[...], raw.astype(BF16), preferred_element_type=F32)
        inverse = 1.0 / attended[128:129]
        delta = jnp.sum(gt_ref[:, here] * attended[0:128], axis=0, keepdims=True) * inverse
        score_grad = (raw * (nt(v_ref[...], g_ref[here]) - delta)).astype(BF16)
        dq = jnp.dot(kt_ref[...], score_grad, preferred_element_type=F32) * (inverse * SCALE)
        dq_ref[here] = dq.T
        dk = nt(score_grad, (qt_ref[:, here].astype(F32) * inverse).astype(BF16))
        if i == 0:
            dk_ref[...] = dk
        else:
            dk_ref[...] += dk

    dq = dq_ref[...].astype(BF16)
    dk = (dk_ref[...] * SCALE).astype(BF16)
    for s in range(WAYS):
        for n, grad in enumerate((dq, dk)):
            block = grad[s * TOK_DEV : (s + 1) * TOK_DEV]
            out_ref[s, n * 16 : (n + 1) * 16] = block[TAIL:]
            out_ref[s, BACK_HEAD + n * TAIL : BACK_HEAD + (n + 1) * TAIL] = block[:TAIL]

    def total(grad, norm, gain_ref):
        summed = jnp.sum(grad.astype(F32) * norm.astype(F32), axis=0, keepdims=True)
        return summed / gain_ref[pl.ds(slot * HEADS + head, 1)]

    gain_ref[pl.ds(head, 1)] = total(dq, q_ref[:, 0:128], qg_ref)
    gain_ref[pl.ds(HEADS + head, 1)] = total(dk, k_ref[:, 0:128], kg_ref)


def whole_block(shape):
    return pl.BlockSpec(shape, lambda b: (0,) * len(shape))


def attention(res_len, blocks, q_gain, k_gain):
    return pl.pallas_call(
        attention_kernel,
        grid=(HEADS,),
        in_specs=[SMEM, pl.BlockSpec((WAYS, SENT, 128), lambda b: (0, 0, b))]
        + [whole_block((BLOCKS, 128))] * 2,
        out_specs=[
            pl.BlockSpec((WAYS, BACK, 128), lambda b: (0, 0, b)),
            whole_block((8, 128)),
        ],
        out_shape=[
            jax.ShapeDtypeStruct((WAYS, BACK, LOCAL), BF16),
            jax.ShapeDtypeStruct((8, 128), F32),
        ],
        scratch_shapes=[pltpu.VMEM((ALL, 256), BF16)] * 2
        + [pltpu.VMEM((ALL, 128), BF16)] * 2
        + [pltpu.VMEM((128, ALL), BF16)] * 2
        + [pltpu.VMEM((128 + ONES, ALL), BF16), pltpu.VMEM((128, ALL), F32)]
        + [pltpu.VMEM((ALL, 128), F32)] * 2,
        compiler_params=params(1),
        cost_estimate=pl.CostEstimate(
            flops=4_000_000_000, bytes_accessed=5_000_000, transcendentals=3_200_000
        ),
        name="attention",
    )(res_len, blocks, q_gain, k_gain)


def short_kernel(
    dest_ref, move_ref, parts_ref, g_ref, grad_ref, part_ref, qg_ref, kg_ref, out_ref, gain_ref
):
    head = pl.program_id(0)
    slot = lax.axis_index("head")
    move_len = move_ref[find_source(dest_ref, lax.axis_index("dp"))]
    count = WAYS * MOV
    lane = lax.broadcasted_iota(jnp.int32, (1, count), 1)
    bias = jnp.where(lane < move_len, 0.0, -1e30).astype(F32)

    def gathered(n):
        return parts_ref[pl.ds((n * HEADS + head) * PAIRS, PAIRS)].reshape(count, 128)

    def per_device(rows):
        return rows.reshape(WAYS, MOV, 128)

    q, k, v = gathered(0), gathered(1), gathered(2)
    q_float, k_float = q.astype(F32), k.astype(F32)
    weighted = g_ref[...].astype(F32)[:, 8:16].reshape(count, 128)
    dq, dk = grads(q, k, v, weighted.astype(BF16), bias)
    dq = dq.astype(BF16).astype(F32)
    dk = (dk * SCALE).astype(BF16).astype(F32)
    for n, grad in enumerate((dq, dk)):
        kept = grad_ref[:, n * 16 : (n + 1) * 16].astype(F32)[:, 0:8]
        both = jnp.concatenate([kept, per_device(grad)], axis=1)
        out_ref[:, n * 16 : (n + 1) * 16] = both.astype(BF16)
    norms = jnp.concatenate([per_device(q_float), per_device(k_float)], axis=1)
    out_ref[:, BACK_MORE : BACK_MORE + 16] = norms.astype(BF16)
    scales = parts_ref[SCALES : SCALES + PAIRS].astype(F32).reshape(WAYS, MOV, 128)
    scales = jnp.concatenate([scales, jnp.zeros_like(scales)], axis=1)
    out_ref[:, BACK_MORE + 16 : BACK_HEAD] = scales.astype(BF16)

    @pl.when(head == 0)
    def _():
        gain_ref[...] = part_ref[...]

    def total(grad, norm, gains):
        return jnp.sum(grad * norm, axis=0, keepdims=True) / gains[pl.ds(slot * HEADS + head, 1)]

    gain_ref[pl.ds(head, 1)] += total(dq, q_float, qg_ref)
    gain_ref[pl.ds(HEADS + head, 1)] += total(dk, k_float, kg_ref)


def short_attention(dest, move_len, parts, blocks, grad, part, q_gain, k_gain):
    head_rows = pl.BlockSpec((WAYS, BACK_HEAD, 128), lambda b: (0, 0, b))
    return pl.pallas_call(
        short_kernel,
        grid=(HEADS,),
        in_specs=[SMEM] * 2
        + [whole_block((GROUPS, 16, 128))]
        + [pl.BlockSpec((WAYS, 16, 128), lambda b: (0, (EXTRA - 16) // 16, b))]
        + [head_rows, whole_block((8, 128))]
        + [whole_block((BLOCKS, 128))] * 2,
        out_specs=[head_rows, whole_block((8, 128))],
        out_shape=[
            jax.ShapeDtypeStruct(grad.shape, BF16),
            jax.ShapeDtypeStruct((8, 128), F32),
        ],
        input_output_aliases={4: 0},
        compiler_params=params(1),
        cost_estimate=pl.CostEstimate(
            flops=20_000_000, bytes_accessed=1_000_000, transcendentals=12_000
        ),
        name="short_attention",
    )(dest, move_len, parts, blocks, grad, part, q_gain, k_gain)


POST_ROWS = 16


def post_kernel(
    q_ref, k_ref, more_ref, qg_ref, kg_ref, dq_ref, dk_ref, oq_ref, ok_ref, unit_ref, scale_ref
):
    last = pl.program_id(0) == TOK_DEV // POST_ROWS - 1

    def one(n, in_ref, gain_ref, grad_ref, out_ref):
        x = in_ref[...].astype(F32)
        scale = row_scale(x)
        scale_ref[...] = jnp.broadcast_to(scale, scale_ref.shape)
        unit_ref[...] = x * scale
        gain = gain_ref[...]

        @pl.when(last)
        def _():
            norms = jnp.concatenate(
                [more_ref[p, 0:16].astype(F32)[n * 8 : n * 8 + 8] for p in range(WAYS)], axis=1
            )
            unit_ref[8:16] = norms / gain
            terms = more_ref[0, 16:32, 0:128].astype(F32)[0:8]
            total = terms[:, 2 * n : 2 * n + 1] + terms[:, 2 * n + 1 : 2 * n + 2]
            scale_ref[8:16] = jnp.broadcast_to(total, (8, 128))

        unit = unit_ref[...]
        grad = jnp.concatenate([grad_ref[p].astype(F32) for p in range(WAYS)], axis=1) * gain
        dots = jnp.sum(unit * grad, axis=1, keepdims=True) / HD
        out_ref[...] = (scale_ref[:, 0:1] * (grad - unit * dots)).astype(BF16)

    one(0, q_ref, qg_ref, dq_ref, oq_ref)
    one(1, k_ref, kg_ref, dk_ref, ok_ref)


def finish(q_in, k_in, q_gain, k_gain, back):
    rows = pl.BlockSpec((POST_ROWS, HD), lambda i: (i, 0))
    gain = pl.BlockSpec((1, HD), lambda i: (0, 0))
    steps = TOK_DEV // POST_ROWS

    def grad_rows(n):
        first = (BACK_HEAD + n * TAIL) // 16
        return pl.BlockSpec(
            (WAYS, 16, LOCAL), lambda i: (0, jnp.where(i == steps - 1, n, first + i), 0)
        )

    return pl.pallas_call(
        post_kernel,
        grid=(steps,),
        in_specs=[
            rows,
            rows,
            pl.BlockSpec((WAYS, 32, LOCAL), lambda i: (0, BACK_MORE // 32, 0)),
            gain,
            gain,
            grad_rows(0),
            grad_rows(1),
        ],
        out_specs=[rows, rows],
        out_shape=[jax.ShapeDtypeStruct((TOK_DEV, HD), BF16)] * 2,
        scratch_shapes=[pltpu.VMEM((POST_ROWS, HD), F32), pltpu.VMEM((POST_ROWS, 128), F32)],
        compiler_params=params(1),
        cost_estimate=pl.CostEstimate(flops=20_000_000, bytes_accessed=4_800_000, transcendentals=0),
        name="finish",
    )(q_in, k_in, back, q_gain, k_gain, back, back)


def swap_all(x, axis):
    return lax.all_to_all(x, axis, split_axis=0, concat_axis=0, tiled=True)


def gather_sum(x, rings):
    return jnp.sum(lax.all_gather(x, "dp", axis_index_groups=rings), axis=0)


def local(
    q_in, k_in, v_in, grad_out, q_gain, k_gain,
    res_len, move_len, step_index, dest_group, loss_weight,
):
    gain_q, gain_k = q_gain.reshape(1, HD), k_gain.reshape(1, HD)
    gain_q_rows, gain_k_rows = q_gain.reshape(BLOCKS, 128), k_gain.reshape(BLOCKS, 128)
    sent = prepare(
        dest_group, res_len, move_len, step_index, loss_weight,
        q_in, k_in, v_in, grad_out, gain_q, gain_k,
    )
    blocks = swap_all(sent, "head")
    packed, blocks = lax.optimization_barrier((pack_short(blocks), blocks))
    spread = swap_all(packed, "dp")
    grad, part = attention(res_len, blocks, gain_q_rows, gain_k_rows)
    spread, part = lax.optimization_barrier((spread, part))
    parts = swap_all(scatter_short(dest_group, spread), "dp")
    grad, part = short_attention(
        dest_group, move_len, parts, blocks, grad, part, gain_q_rows, gain_k_rows
    )
    back = swap_all(grad, "head")
    total = gather_sum(gather_sum(part, ZRING), PLANE)
    out_q, out_k = finish(q_in, k_in, gain_q, gain_k, back)
    return (
        out_q,
        out_k,
        total[:HEADS].reshape(LOCAL),
        total[HEADS : 2 * HEADS].reshape(LOCAL),
    )


def solution(mesh):
    tokens = P(("dp", "head"), None)
    return jax.shard_map(
        local,
        mesh=mesh,
        in_specs=(tokens,) * 4 + (P(),) * 7,
        out_specs=(tokens, tokens, P("head"), P("head")),
        check_vma=False,
    )
```

```python
import math

import jax
import jax.numpy as jnp
from jax import lax
from jax.experimental import pallas as pl
from jax.experimental.pallas import tpu as pltpu
from jax.sharding import PartitionSpec as P

HEAD_DIM = 128
TOK_DEV = 128
MOV = 8
RES = 120
EPS = 1e-06
WAYS = 8
GROUPS = 64
HD = 3072
LOCAL = HD // WAYS
HEADS = LOCAL // HEAD_DIM
BLOCKS = HD // 128
SCALE = 1.0 / math.sqrt(HEAD_DIM)
F32 = jnp.float32
BF16 = jnp.bfloat16
VMEM_LIMIT = 63 * 1024 * 1024

PLANE = [[xl * 32 + z * 2 + c for xl in range(2) for c in range(2)] for z in range(16)]
ZRING = [[xl * 32 + z * 2 + c for z in range(16)] for xl in range(2) for c in range(2)]

SMEM = pl.BlockSpec(memory_space=pltpu.SMEM)


def params(count=0):
    return pltpu.CompilerParams(
        vmem_limit_bytes=VMEM_LIMIT,
        dimension_semantics=("arbitrary",) * count if count else None,
    )


def find_source(dest_ref, group):
    return lax.fori_loop(
        0, GROUPS, lambda g, found: jnp.where(dest_ref[g] == group, g, found), jnp.int32(0)
    )


def pack_kernel(q_ref, k_ref, v_ref, out_ref):
    q = q_ref[...].astype(F32)[8:16]
    k = k_ref[...].astype(F32)[8:16]
    v = v_ref[...].astype(F32)[8:16]
    pair = jnp.concatenate([q, k], axis=0).astype(BF16)
    half = HD // 2
    tail = jnp.concatenate([v[:, :half], v[:, half:]], axis=0).astype(BF16)
    for c in range(BLOCKS):
        out_ref[c] = pair[:, c * 128 : (c + 1) * 128]
    for c in range(BLOCKS // 2):
        out_ref[BLOCKS + c] = tail[:, c * 128 : (c + 1) * 128]
    rest = GROUPS - BLOCKS - BLOCKS // 2
    out_ref[pl.ds(BLOCKS + BLOCKS // 2, rest)] = jnp.zeros((rest, 16, 128), BF16)


def pack_short(q_in, k_in, v_in):
    spec = pl.BlockSpec((16, HD), lambda i: (TOK_DEV // 16 - 1, 0))
    return pl.pallas_call(
        pack_kernel,
        grid=(1,),
        in_specs=[spec] * 3,
        out_specs=pl.BlockSpec((GROUPS, 16, 128), lambda i: (0, 0, 0)),
        out_shape=jax.ShapeDtypeStruct((GROUPS, 16, 128), BF16),
        compiler_params=params(1),
        name="pack_short",
    )(q_in, k_in, v_in)


def scatter_kernel(dest_ref, in_ref, out_ref):
    def step(g, carry):
        out_ref[dest_ref[g]] = in_ref[g]
        return carry

    lax.fori_loop(0, GROUPS, step, 0)


def scatter_short(dest_group, parts):
    whole = pl.BlockSpec(memory_space=pltpu.VMEM)
    return pl.pallas_call(
        scatter_kernel,
        in_specs=[SMEM, whole],
        out_specs=whole,
        out_shape=jax.ShapeDtypeStruct(parts.shape, BF16),
        compiler_params=params(),
        name="scatter_short",
    )(dest_group, parts)


def norm_rows(rows, gain):
    scale = lax.rsqrt(jnp.sum(rows * rows, axis=1, keepdims=True) / HD + EPS)
    return rows * scale * gain


def unpack_kernel(in_ref, qg_ref, kg_ref, send_ref, raw_ref):
    pair = jnp.concatenate([in_ref[c] for c in range(BLOCKS)], axis=1).astype(F32)
    tail = jnp.concatenate([in_ref[BLOCKS + c] for c in range(BLOCKS // 2)], axis=1).astype(F32)
    q, k = pair[0:8], pair[8:16]
    v = jnp.concatenate([tail[0:8], tail[8:16]], axis=1)
    qn = norm_rows(q, qg_ref[...])
    kn = norm_rows(k, kg_ref[...])
    zero = jnp.zeros((8, HD), F32)
    first = jnp.concatenate([qn, kn], axis=0).astype(BF16)
    second = jnp.concatenate([v, zero], axis=0).astype(BF16)
    for p in range(WAYS):
        send_ref[p, 0:16, :] = first[:, p * LOCAL : (p + 1) * LOCAL]
        send_ref[p, 16:32, :] = second[:, p * LOCAL : (p + 1) * LOCAL]
    raw_ref[0] = jnp.concatenate([zero, q], axis=0).astype(BF16)
    raw_ref[1] = jnp.concatenate([zero, k], axis=0).astype(BF16)


def unpack_short(parts, q_gain, k_gain):
    whole = pl.BlockSpec(memory_space=pltpu.VMEM)
    return pl.pallas_call(
        unpack_kernel,
        in_specs=[whole] * 3,
        out_specs=[whole] * 2,
        out_shape=[
            jax.ShapeDtypeStruct((WAYS, 32, LOCAL), BF16),
            jax.ShapeDtypeStruct((2, 16, HD), BF16),
        ],
        compiler_params=params(),
        name="unpack_short",
    )(parts, q_gain, k_gain)


PRE_ROWS = 64


def pre_kernel(
    dest_ref, res_ref, move_ref, step_ref, table_ref,
    q_ref, k_ref, v_ref, go_ref, qg_ref, kg_ref,
    *rest,
):
    outs, (qn_ref, kn_ref) = rest[:WAYS], rest[WAYS:]
    group = lax.axis_index("dp")
    slot = lax.axis_index("head")
    source = find_source(dest_ref, group)
    stay_weight = table_ref[step_ref[group]]
    move_weight = table_ref[step_ref[GROUPS + source]]
    rows = pl.program_id(0) * PRE_ROWS + lax.broadcasted_iota(jnp.int32, (PRE_ROWS, 1), 0)
    stay = jnp.where(slot * RES + rows < res_ref[group], stay_weight, 0.0)
    move = jnp.where(slot * MOV + rows - RES < move_ref[source], move_weight, 0.0)
    weight = jnp.where(rows < RES, stay, move)
    qn_ref[...] = norm_rows(q_ref[...].astype(F32), qg_ref[...]).astype(BF16)
    kn_ref[...] = norm_rows(k_ref[...].astype(F32), kg_ref[...]).astype(BF16)
    for s in range(WAYS):
        start = pl.multiple_of(jnp.bitwise_xor(slot, s) * LOCAL, 128)
        cols = pl.ds(start, LOCAL)
        outs[s][0] = qn_ref[:, cols]
        outs[s][1] = kn_ref[:, cols]
        outs[s][2] = v_ref[:, cols]
        outs[s][3] = (go_ref[:, cols].astype(F32) * weight).astype(BF16)


def prepare(dest, res_len, move_len, steps, table, q_in, k_in, v_in, grad_out, q_gain, k_gain):
    rows = pl.BlockSpec((PRE_ROWS, HD), lambda i: (i, 0))
    gain = pl.BlockSpec((1, HD), lambda i: (0, 0))
    return pl.pallas_call(
        pre_kernel,
        grid=(TOK_DEV // PRE_ROWS,),
        in_specs=[SMEM] * 5 + [rows] * 4 + [gain] * 2,
        out_specs=[pl.BlockSpec((4, PRE_ROWS, LOCAL), lambda i: (0, i, 0))] * WAYS,
        out_shape=[jax.ShapeDtypeStruct((4, TOK_DEV, LOCAL), BF16)] * WAYS,
        scratch_shapes=[pltpu.VMEM((PRE_ROWS, HD), BF16)] * 2,
        compiler_params=params(1),
        cost_estimate=pl.CostEstimate(flops=20_000_000, bytes_accessed=6_300_000, transcendentals=0),
        name="prepare",
    )(dest, res_len, move_len, steps, table, q_in, k_in, v_in, grad_out, q_gain, k_gain)


def nt(a, b):
    return lax.dot_general(a, b, (((1,), (1,)), ((), ())), preferred_element_type=F32)


def tn(a, b):
    return lax.dot_general(a, b, (((0,), (0,)), ((), ())), preferred_element_type=F32)


def grads(q, k, v, g, bias):
    scores = nt(q, k) * SCALE + bias
    top = jnp.max(scores, axis=1, keepdims=True)
    raw = jnp.exp(scores - top)
    weights = raw * (1.0 / jnp.sum(raw, axis=1, keepdims=True))
    attended = jnp.dot(weights.astype(BF16), v, preferred_element_type=F32)
    delta = jnp.sum(g.astype(F32) * attended, axis=1, keepdims=True)
    score_grad = (weights * (nt(g, v) - delta)).astype(BF16)
    query_grad = jnp.dot(score_grad, k, preferred_element_type=F32) * SCALE
    return query_grad, tn(score_grad, q)


QUERY_ROWS = 512
ALL = WAYS * TOK_DEV
ONES = 16
POWER = SCALE * math.log2(math.e)


def flip(block):
    return block.astype(F32).T.astype(BF16)


TAIL = TOK_DEV - 16


def attention_kernel(res_ref, *rest):
    slots, rest = rest[:WAYS], rest[WAYS:]
    qg_ref, kg_ref, out_ref, gain_ref, short_g_ref, *rest = rest
    q_ref, k_ref, v_ref, g_ref, qt_ref, kt_ref, vt_ref, gt_ref, dq_ref, dk_ref = rest
    head = pl.program_id(0)
    slot = lax.axis_index("head")
    stay_len = res_ref[lax.axis_index("dp")]
    peers = [jnp.bitwise_xor(slot, s) for s in range(WAYS)]
    rows = lax.broadcasted_iota(jnp.int32, (TOK_DEV, 1), 0)
    first_lane = lax.broadcasted_iota(jnp.int32, (TOK_DEV, 128), 1) == 0
    for s in range(WAYS):
        here = pl.ds(s * TOK_DEV, TOK_DEV)
        q, k, v, g = (slots[s][n] for n in range(4))
        short_g_ref[peers[s]] = g[TAIL:]
        g = jnp.where(rows < RES, g.astype(F32), 0.0)
        limit = jnp.minimum(stay_len - peers[s] * RES, RES)
        q_ref[here, 0:128] = q
        q_ref[here, 128:256] = jnp.where(first_lane, 1.0, 0.0).astype(BF16)
        k_ref[here, 0:128] = k
        masked = jnp.logical_and(first_lane, rows >= limit)
        k_ref[here, 128:256] = jnp.where(masked, -1e30, 0.0).astype(BF16)
        v_ref[here] = v
        g_ref[here] = g.astype(BF16)
        qt_ref[:, here] = flip(q)
        kt_ref[:, here] = flip(k)
        vt_ref[0:128, here] = flip(v)
        gt_ref[:, here] = g.T
    ones = lax.broadcasted_iota(jnp.int32, (ONES, ALL), 0) == 0
    vt_ref[128 : 128 + ONES, :] = jnp.where(ones, 1.0, 0.0).astype(BF16)

    for i in range(ALL // QUERY_ROWS):
        here = pl.ds(i * QUERY_ROWS, QUERY_ROWS)
        scores = nt(k_ref[...], q_ref[here])
        raw = jnp.exp2((scores - jnp.max(scores, axis=0, keepdims=True)) * POWER)
        attended = jnp.dot(vt_ref[...], raw.astype(BF16), preferred_element_type=F32)
        inverse = 1.0 / attended[128:129]
        delta = jnp.sum(gt_ref[:, here] * attended[0:128], axis=0, keepdims=True) * inverse
        score_grad = (raw * (nt(v_ref[...], g_ref[here]) - delta)).astype(BF16)
        dq = jnp.dot(kt_ref[...], score_grad, preferred_element_type=F32) * (inverse * SCALE)
        dq_ref[here] = dq.T
        dk = nt(score_grad, (qt_ref[:, here].astype(F32) * inverse).astype(BF16))
        if i == 0:
            dk_ref[...] = dk
        else:
            dk_ref[...] += dk

    dq = dq_ref[...].astype(BF16)
    dk = (dk_ref[...] * SCALE).astype(BF16)
    for s in range(WAYS):
        for n, grad in enumerate((dq, dk)):
            block = grad[s * TOK_DEV : (s + 1) * TOK_DEV]
            out_ref[peers[s], n] = block

    def total(grad, norm, gain_ref):
        summed = jnp.sum(grad.astype(F32) * norm.astype(F32), axis=0, keepdims=True)
        return summed / gain_ref[pl.ds(slot * HEADS + head, 1)]

    gain_ref[pl.ds(head, 1)] = total(dq, q_ref[:, 0:128], qg_ref)
    gain_ref[pl.ds(HEADS + head, 1)] = total(dk, k_ref[:, 0:128], kg_ref)


def whole_block(shape):
    return pl.BlockSpec(shape, lambda b: (0,) * len(shape))


def attention(res_len, slots, q_gain, k_gain):
    return pl.pallas_call(
        attention_kernel,
        grid=(HEADS,),
        in_specs=[SMEM]
        + [pl.BlockSpec((4, TOK_DEV, 128), lambda b: (0, 0, b))] * WAYS
        + [whole_block((BLOCKS, 128))] * 2,
        out_specs=[
            pl.BlockSpec((WAYS, 2, TOK_DEV, 128), lambda b: (0, 0, 0, b)),
            whole_block((8, 128)),
            pl.BlockSpec((WAYS, 16, 128), lambda b: (0, 0, b)),
        ],
        out_shape=[
            jax.ShapeDtypeStruct((WAYS, 2, TOK_DEV, LOCAL), BF16),
            jax.ShapeDtypeStruct((8, 128), F32),
            jax.ShapeDtypeStruct((WAYS, 16, LOCAL), BF16),
        ],
        scratch_shapes=[pltpu.VMEM((ALL, 256), BF16)] * 2
        + [pltpu.VMEM((ALL, 128), BF16)] * 2
        + [pltpu.VMEM((128, ALL), BF16)] * 2
        + [pltpu.VMEM((128 + ONES, ALL), BF16), pltpu.VMEM((128, ALL), F32)]
        + [pltpu.VMEM((ALL, 128), F32)] * 2,
        compiler_params=params(1),
        cost_estimate=pl.CostEstimate(
            flops=4_000_000_000, bytes_accessed=5_000_000, transcendentals=3_200_000
        ),
        name="attention",
    )(res_len, *slots, q_gain, k_gain)


def short_kernel(
    dest_ref, move_ref, short_ref, g_ref, grad_ref, part_ref, qg_ref, kg_ref, out_ref, gain_ref
):
    slot = lax.axis_index("head")
    move_len = move_ref[find_source(dest_ref, lax.axis_index("dp"))]
    count = WAYS * MOV
    lane = lax.broadcasted_iota(jnp.int32, (1, count), 1)
    bias = jnp.where(lane < move_len, 0.0, -1e30).astype(F32)
    gain_ref[...] = part_ref[...]

    def rows_at(values, first):
        return values[:, first : first + MOV].reshape(count, 128)

    for head in range(HEADS):
        cols = slice(head * 128, (head + 1) * 128)
        lines = short_ref[:, :, cols].astype(F32)
        q, k, v = rows_at(lines, 0), rows_at(lines, 8), rows_at(lines, 16)
        g = rows_at(g_ref[:, :, cols].astype(F32), 8)
        dq, dk = grads(q.astype(BF16), k.astype(BF16), v.astype(BF16), g.astype(BF16), bias)
        dq = dq.astype(BF16).astype(F32)
        dk = (dk * SCALE).astype(BF16).astype(F32)
        for n, grad, norm, gains in ((0, dq, q, qg_ref), (1, dk, k, kg_ref)):
            kept = grad_ref[:, n, :, cols].astype(F32)[:, 0:8]
            both = jnp.concatenate([kept, grad.reshape(WAYS, MOV, 128)], axis=1)
            out_ref[:, n, :, cols] = both.astype(BF16)
            total = jnp.sum(grad * norm, axis=0, keepdims=True)
            total = total / gains[pl.ds(slot * HEADS + head, 1)]
            gain_ref[n * HEADS + head : n * HEADS + head + 1] += total


def short_attention(dest, move_len, short, short_g, grad, part, q_gain, k_gain):
    tail = pl.BlockSpec((WAYS, 2, 16, LOCAL), lambda i: (0, 0, TAIL // 16, 0))
    return pl.pallas_call(
        short_kernel,
        grid=(1,),
        in_specs=[SMEM] * 2
        + [whole_block((WAYS, 32, LOCAL)), whole_block((WAYS, 16, LOCAL))]
        + [tail, whole_block((8, 128))]
        + [whole_block((BLOCKS, 128))] * 2,
        out_specs=[tail, whole_block((8, 128))],
        out_shape=[
            jax.ShapeDtypeStruct(grad.shape, BF16),
            jax.ShapeDtypeStruct((8, 128), F32),
        ],
        input_output_aliases={4: 0},
        compiler_params=params(1),
        cost_estimate=pl.CostEstimate(
            flops=20_000_000, bytes_accessed=1_000_000, transcendentals=12_000
        ),
        name="short_attention",
    )(dest, move_len, short, short_g, grad, part, q_gain, k_gain)


POST_ROWS = 64


def post_kernel(q_ref, k_ref, raw_ref, qg_ref, kg_ref, dq_ref, dk_ref, oq_ref, ok_ref):
    last = pl.program_id(0) == TOK_DEV // POST_ROWS - 1
    row = lax.broadcasted_iota(jnp.int32, (POST_ROWS, 1), 0)
    use_short = jnp.logical_and(last, row >= POST_ROWS - MOV)

    def one(in_ref, which, gain_ref, grad_ref, out_ref):
        short = raw_ref[which].astype(F32)
        short = jnp.concatenate([jnp.zeros((POST_ROWS - 16, HD), F32), short], axis=0)
        x = jnp.where(use_short, short, in_ref[...].astype(F32))
        scale = lax.rsqrt(jnp.sum(x * x, axis=1, keepdims=True) / HD + EPS)
        gain = gain_ref[...]
        grad = jnp.concatenate([grad_ref[p, 0].astype(F32) for p in range(WAYS)], axis=1) * gain
        dots = jnp.sum(x * grad, axis=1, keepdims=True)
        out_ref[...] = (scale * grad - x * ((scale * scale * scale) * dots / HD)).astype(BF16)

    one(q_ref, 0, qg_ref, dq_ref, oq_ref)
    one(k_ref, 1, kg_ref, dk_ref, ok_ref)


def finish(q_in, k_in, raw, q_gain, k_gain, back):
    rows = pl.BlockSpec((POST_ROWS, HD), lambda i: (i, 0))
    gain = pl.BlockSpec((1, HD), lambda i: (0, 0))
    return pl.pallas_call(
        post_kernel,
        grid=(TOK_DEV // POST_ROWS,),
        in_specs=[
            rows,
            rows,
            pl.BlockSpec((2, 16, HD), lambda i: (0, 0, 0)),
            gain,
            gain,
            pl.BlockSpec((WAYS, 1, POST_ROWS, LOCAL), lambda i: (0, 0, i, 0)),
            pl.BlockSpec((WAYS, 1, POST_ROWS, LOCAL), lambda i: (0, 1, i, 0)),
        ],
        out_specs=[rows, rows],
        out_shape=[jax.ShapeDtypeStruct((TOK_DEV, HD), BF16)] * 2,
        compiler_params=params(1),
        cost_estimate=pl.CostEstimate(flops=20_000_000, bytes_accessed=4_800_000, transcendentals=0),
        name="finish",
    )(q_in, k_in, raw, q_gain, k_gain, back, back)


EARLY = (4, 1)
LATE = (6, 3, 5, 2, 7)


def swap_all(x, axis):
    return lax.all_to_all(x, axis, split_axis=0, concat_axis=0, tiled=True)


def gather_sum(x, rings):
    return jnp.sum(lax.all_gather(x, "dp", axis_index_groups=rings), axis=0)


def local(
    q_in, k_in, v_in, grad_out, q_gain, k_gain,
    res_len, move_len, step_index, dest_group, loss_weight,
):
    gain_q, gain_k = q_gain.reshape(1, HD), k_gain.reshape(1, HD)
    packed, grad_rows = lax.optimization_barrier((pack_short(q_in, k_in, v_in), grad_out))
    spread = swap_all(packed, "dp")
    own, *outgoing = prepare(
        dest_group, res_len, move_len, step_index.T.reshape(2 * GROUPS), loss_weight,
        q_in, k_in, v_in, grad_rows, gain_q, gain_k,
    )
    slots = {0: own}
    for n in EARLY + LATE:
        slots[n] = lax.ppermute(outgoing[n - 1], "head", [(i, i ^ n) for i in range(WAYS)])
    spread, *held = lax.optimization_barrier((spread, *(slots[n] for n in EARLY)))
    slots.update(zip(EARLY, held, strict=True))
    routed = swap_all(scatter_short(dest_group, spread), "dp")
    short, raw = unpack_short(routed, gain_q, gain_k)
    short = swap_all(short, "head")
    gain_q_rows, gain_k_rows = q_gain.reshape(BLOCKS, 128), k_gain.reshape(BLOCKS, 128)
    grad, part, short_g = attention(
        res_len, [slots[n] for n in range(WAYS)], gain_q_rows, gain_k_rows
    )
    grad, part = short_attention(
        dest_group, move_len, short, short_g, grad, part, gain_q_rows, gain_k_rows
    )
    back = swap_all(grad, "head")
    total = gather_sum(gather_sum(part, ZRING), PLANE)
    out_q, out_k = finish(q_in, k_in, raw, gain_q, gain_k, back)
    return (
        out_q,
        out_k,
        total[:HEADS].reshape(LOCAL),
        total[HEADS : 2 * HEADS].reshape(LOCAL),
    )


def solution(mesh):
    tokens = P(("dp", "head"), None)
    return jax.shard_map(
        local,
        mesh=mesh,
        in_specs=(tokens,) * 4 + (P(),) * 7,
        out_specs=(tokens, tokens, P("head"), P("head")),
        check_vma=False,
    )
```

```python
import math

import jax
import jax.numpy as jnp
from jax import lax
from jax.experimental import pallas as pl
from jax.experimental.pallas import tpu as pltpu
from jax.sharding import PartitionSpec as P

HEAD_DIM = 128
TOK_DEV = 128
MOV = 8
RES = 120
EPS = 1e-06
WAYS = 8
GROUPS = 64
HD = 3072
LOCAL = HD // WAYS
HEADS = LOCAL // HEAD_DIM
BLOCKS = HD // 128
SCALE = 1.0 / math.sqrt(HEAD_DIM)
F32 = jnp.float32
BF16 = jnp.bfloat16
VMEM_LIMIT = 63 * 1024 * 1024

PLANE = [[xl * 32 + z * 2 + c for xl in range(2) for c in range(2)] for z in range(16)]
ZRING = [[xl * 32 + z * 2 + c for z in range(16)] for xl in range(2) for c in range(2)]

SMEM = pl.BlockSpec(memory_space=pltpu.SMEM)


def params(count=0):
    return pltpu.CompilerParams(
        vmem_limit_bytes=VMEM_LIMIT,
        dimension_semantics=("arbitrary",) * count if count else None,
    )


def find_source(dest_ref, group):
    return lax.fori_loop(
        0, GROUPS, lambda g, found: jnp.where(dest_ref[g] == group, g, found), jnp.int32(0)
    )


def pack_kernel(q_ref, k_ref, v_ref, out_ref):
    q = q_ref[...].astype(F32)[8:16]
    k = k_ref[...].astype(F32)[8:16]
    v = v_ref[...].astype(F32)[8:16]
    pair = jnp.concatenate([q, k], axis=0).astype(BF16)
    half = HD // 2
    tail = jnp.concatenate([v[:, :half], v[:, half:]], axis=0).astype(BF16)
    for c in range(BLOCKS):
        out_ref[c] = pair[:, c * 128 : (c + 1) * 128]
    for c in range(BLOCKS // 2):
        out_ref[BLOCKS + c] = tail[:, c * 128 : (c + 1) * 128]
    rest = GROUPS - BLOCKS - BLOCKS // 2
    out_ref[pl.ds(BLOCKS + BLOCKS // 2, rest)] = jnp.zeros((rest, 16, 128), BF16)


def pack_short(q_in, k_in, v_in):
    spec = pl.BlockSpec((16, HD), lambda i: (TOK_DEV // 16 - 1, 0))
    return pl.pallas_call(
        pack_kernel,
        grid=(1,),
        in_specs=[spec] * 3,
        out_specs=pl.BlockSpec((GROUPS, 16, 128), lambda i: (0, 0, 0)),
        out_shape=jax.ShapeDtypeStruct((GROUPS, 16, 128), BF16),
        compiler_params=params(1),
        name="pack_short",
    )(q_in, k_in, v_in)


def scatter_kernel(dest_ref, in_ref, out_ref):
    def step(g, carry):
        out_ref[dest_ref[g]] = in_ref[g]
        return carry

    lax.fori_loop(0, GROUPS, step, 0)


def scatter_short(dest_group, parts):
    whole = pl.BlockSpec(memory_space=pltpu.VMEM)
    return pl.pallas_call(
        scatter_kernel,
        in_specs=[SMEM, whole],
        out_specs=whole,
        out_shape=jax.ShapeDtypeStruct(parts.shape, BF16),
        compiler_params=params(),
        name="scatter_short",
    )(dest_group, parts)


def norm_rows(rows, gain):
    scale = lax.rsqrt(jnp.sum(rows * rows, axis=1, keepdims=True) / HD + EPS)
    return rows * scale * gain


def unpack_kernel(
    dest_ref, move_ref, step_ref, table_ref, in_ref, go_ref, qg_ref, kg_ref, send_ref, raw_ref
):
    slot = lax.axis_index("head")
    source = find_source(dest_ref, lax.axis_index("dp"))
    position = slot * MOV + lax.broadcasted_iota(jnp.int32, (MOV, 1), 0)
    weight = jnp.where(position < move_ref[source], table_ref[step_ref[GROUPS + source]], 0.0)
    weighted = go_ref[...].astype(F32)[8:16] * weight
    pair = jnp.concatenate([in_ref[c] for c in range(BLOCKS)], axis=1).astype(F32)
    tail = jnp.concatenate([in_ref[BLOCKS + c] for c in range(BLOCKS // 2)], axis=1).astype(F32)
    q, k = pair[0:8], pair[8:16]
    v = jnp.concatenate([tail[0:8], tail[8:16]], axis=1)
    qn = norm_rows(q, qg_ref[...])
    kn = norm_rows(k, kg_ref[...])
    zero = jnp.zeros((8, HD), F32)
    first = jnp.concatenate([qn, kn], axis=0).astype(BF16)
    second = jnp.concatenate([v, weighted], axis=0).astype(BF16)
    for p in range(WAYS):
        send_ref[p, 0:16, :] = first[:, p * LOCAL : (p + 1) * LOCAL]
        send_ref[p, 16:32, :] = second[:, p * LOCAL : (p + 1) * LOCAL]
    raw_ref[0] = jnp.concatenate([zero, q], axis=0).astype(BF16)
    raw_ref[1] = jnp.concatenate([zero, k], axis=0).astype(BF16)


def unpack_short(dest, move_len, steps, table, parts, grad_out, q_gain, k_gain):
    gain = pl.BlockSpec((1, HD), lambda i: (0, 0))
    return pl.pallas_call(
        unpack_kernel,
        grid=(1,),
        in_specs=[SMEM] * 4
        + [pl.BlockSpec((GROUPS, 16, 128), lambda i: (0, 0, 0))]
        + [pl.BlockSpec((16, HD), lambda i: (TOK_DEV // 16 - 1, 0))]
        + [gain] * 2,
        out_specs=[
            pl.BlockSpec((WAYS, 32, LOCAL), lambda i: (0, 0, 0)),
            pl.BlockSpec((2, 16, HD), lambda i: (0, 0, 0)),
        ],
        out_shape=[
            jax.ShapeDtypeStruct((WAYS, 32, LOCAL), BF16),
            jax.ShapeDtypeStruct((2, 16, HD), BF16),
        ],
        compiler_params=params(1),
        name="unpack_short",
    )(dest, move_len, steps, table, parts, grad_out, q_gain, k_gain)


PRE_ROWS = 64


def pre_kernel(
    dest_ref, res_ref, move_ref, step_ref, table_ref,
    q_ref, k_ref, v_ref, go_ref, qg_ref, kg_ref,
    *rest,
):
    outs, (qn_ref, kn_ref) = rest[:WAYS], rest[WAYS:]
    group = lax.axis_index("dp")
    slot = lax.axis_index("head")
    source = find_source(dest_ref, group)
    stay_weight = table_ref[step_ref[group]]
    move_weight = table_ref[step_ref[GROUPS + source]]
    rows = pl.program_id(0) * PRE_ROWS + lax.broadcasted_iota(jnp.int32, (PRE_ROWS, 1), 0)
    stay = jnp.where(slot * RES + rows < res_ref[group], stay_weight, 0.0)
    move = jnp.where(slot * MOV + rows - RES < move_ref[source], move_weight, 0.0)
    weight = jnp.where(rows < RES, stay, move)
    qn_ref[...] = norm_rows(q_ref[...].astype(F32), qg_ref[...]).astype(BF16)
    kn_ref[...] = norm_rows(k_ref[...].astype(F32), kg_ref[...]).astype(BF16)
    for s in range(WAYS):
        start = pl.multiple_of(jnp.bitwise_xor(slot, s) * LOCAL, 128)
        cols = pl.ds(start, LOCAL)
        outs[s][0] = qn_ref[:, cols]
        outs[s][1] = kn_ref[:, cols]
        outs[s][2] = v_ref[:, cols]
        outs[s][3] = (go_ref[:, cols].astype(F32) * weight).astype(BF16)


def prepare(dest, res_len, move_len, steps, table, q_in, k_in, v_in, grad_out, q_gain, k_gain):
    rows = pl.BlockSpec((PRE_ROWS, HD), lambda i: (i, 0))
    gain = pl.BlockSpec((1, HD), lambda i: (0, 0))
    return pl.pallas_call(
        pre_kernel,
        grid=(TOK_DEV // PRE_ROWS,),
        in_specs=[SMEM] * 5 + [rows] * 4 + [gain] * 2,
        out_specs=[pl.BlockSpec((4, PRE_ROWS, LOCAL), lambda i: (0, i, 0))] * WAYS,
        out_shape=[jax.ShapeDtypeStruct((4, TOK_DEV, LOCAL), BF16)] * WAYS,
        scratch_shapes=[pltpu.VMEM((PRE_ROWS, HD), BF16)] * 2,
        compiler_params=params(1),
        cost_estimate=pl.CostEstimate(flops=20_000_000, bytes_accessed=6_300_000, transcendentals=0),
        name="prepare",
    )(dest, res_len, move_len, steps, table, q_in, k_in, v_in, grad_out, q_gain, k_gain)


def nt(a, b):
    return lax.dot_general(a, b, (((1,), (1,)), ((), ())), preferred_element_type=F32)


def tn(a, b):
    return lax.dot_general(a, b, (((0,), (0,)), ((), ())), preferred_element_type=F32)


def grads(q, k, v, g, bias):
    scores = nt(q, k) * SCALE + bias
    top = jnp.max(scores, axis=1, keepdims=True)
    raw = jnp.exp(scores - top)
    weights = raw * (1.0 / jnp.sum(raw, axis=1, keepdims=True))
    attended = jnp.dot(weights.astype(BF16), v, preferred_element_type=F32)
    delta = jnp.sum(g.astype(F32) * attended, axis=1, keepdims=True)
    score_grad = (weights * (nt(g, v) - delta)).astype(BF16)
    query_grad = jnp.dot(score_grad, k, preferred_element_type=F32) * SCALE
    return query_grad, tn(score_grad, q)


QUERY_ROWS = 512
ALL = WAYS * TOK_DEV
ONES = 16
POWER = SCALE * math.log2(math.e)


def flip(block):
    return block.astype(F32).T.astype(BF16)


TAIL = TOK_DEV - 16


def attention_kernel(res_ref, *rest):
    slots, rest = rest[:WAYS], rest[WAYS:]
    short_ref, part_ref, qg_ref, kg_ref, out_ref, gain_ref, *rest = rest
    q_ref, k_ref, v_ref, g_ref, qt_ref, kt_ref, vt_ref, gt_ref, dq_ref, dk_ref = rest
    head = pl.program_id(0)
    slot = lax.axis_index("head")
    stay_len = res_ref[lax.axis_index("dp")]
    peers = [jnp.bitwise_xor(slot, s) for s in range(WAYS)]
    rows = lax.broadcasted_iota(jnp.int32, (TOK_DEV, 1), 0)
    first_lane = lax.broadcasted_iota(jnp.int32, (TOK_DEV, 128), 1) == 0
    for s in range(WAYS):
        here = pl.ds(s * TOK_DEV, TOK_DEV)
        q, k, v, g = (slots[s][n] for n in range(4))
        g = jnp.where(rows < RES, g.astype(F32), 0.0)
        limit = jnp.minimum(stay_len - peers[s] * RES, RES)
        q_ref[here, 0:128] = q
        q_ref[here, 128:256] = jnp.where(first_lane, 1.0, 0.0).astype(BF16)
        k_ref[here, 0:128] = k
        masked = jnp.logical_and(first_lane, rows >= limit)
        k_ref[here, 128:256] = jnp.where(masked, -1e30, 0.0).astype(BF16)
        v_ref[here] = v
        g_ref[here] = g.astype(BF16)
        qt_ref[:, here] = flip(q)
        kt_ref[:, here] = flip(k)
        vt_ref[0:128, here] = flip(v)
        gt_ref[:, here] = g.T
    ones = lax.broadcasted_iota(jnp.int32, (ONES, ALL), 0) == 0
    vt_ref[128 : 128 + ONES, :] = jnp.where(ones, 1.0, 0.0).astype(BF16)

    for i in range(ALL // QUERY_ROWS):
        here = pl.ds(i * QUERY_ROWS, QUERY_ROWS)
        scores = nt(k_ref[...], q_ref[here])
        raw = jnp.exp2((scores - jnp.max(scores, axis=0, keepdims=True)) * POWER)
        attended = jnp.dot(vt_ref[...], raw.astype(BF16), preferred_element_type=F32)
        inverse = 1.0 / attended[128:129]
        delta = jnp.sum(gt_ref[:, here] * attended[0:128], axis=0, keepdims=True) * inverse
        score_grad = (raw * (nt(v_ref[...], g_ref[here]) - delta)).astype(BF16)
        dq = jnp.dot(kt_ref[...], score_grad, preferred_element_type=F32) * (inverse * SCALE)
        dq_ref[here] = dq.T
        dk = nt(score_grad, (qt_ref[:, here].astype(F32) * inverse).astype(BF16))
        if i == 0:
            dk_ref[...] = dk
        else:
            dk_ref[...] += dk

    dq = dq_ref[...].astype(BF16)
    dk = (dk_ref[...] * SCALE).astype(BF16)
    for s in range(WAYS):
        for n, grad in enumerate((dq, dk)):
            block = grad[s * TOK_DEV : (s + 1) * TOK_DEV]
            out_ref[peers[s], n, 0:TAIL] = block[:TAIL]
            tail = block[TAIL:].astype(F32) + short_ref[peers[s], n].astype(F32)
            out_ref[peers[s], n, TAIL:TOK_DEV] = tail.astype(BF16)

    @pl.when(head == 0)
    def _():
        gain_ref[...] = part_ref[...]

    def total(grad, norm, gain_ref):
        summed = jnp.sum(grad.astype(F32) * norm.astype(F32), axis=0, keepdims=True)
        return summed / gain_ref[pl.ds(slot * HEADS + head, 1)]

    gain_ref[pl.ds(head, 1)] += total(dq, q_ref[:, 0:128], qg_ref)
    gain_ref[pl.ds(HEADS + head, 1)] += total(dk, k_ref[:, 0:128], kg_ref)


def whole_block(shape):
    return pl.BlockSpec(shape, lambda b: (0,) * len(shape))


def attention(res_len, slots, short, part, q_gain, k_gain):
    return pl.pallas_call(
        attention_kernel,
        grid=(HEADS,),
        in_specs=[SMEM]
        + [pl.BlockSpec((4, TOK_DEV, 128), lambda b: (0, 0, b))] * WAYS
        + [pl.BlockSpec((WAYS, 2, 16, 128), lambda b: (0, 0, 0, b))]
        + [whole_block((8, 128))]
        + [whole_block((BLOCKS, 128))] * 2,
        out_specs=[
            pl.BlockSpec((WAYS, 2, TOK_DEV, 128), lambda b: (0, 0, 0, b)),
            whole_block((8, 128)),
        ],
        out_shape=[
            jax.ShapeDtypeStruct((WAYS, 2, TOK_DEV, LOCAL), BF16),
            jax.ShapeDtypeStruct((8, 128), F32),
        ],
        scratch_shapes=[pltpu.VMEM((ALL, 256), BF16)] * 2
        + [pltpu.VMEM((ALL, 128), BF16)] * 2
        + [pltpu.VMEM((128, ALL), BF16)] * 2
        + [pltpu.VMEM((128 + ONES, ALL), BF16), pltpu.VMEM((128, ALL), F32)]
        + [pltpu.VMEM((ALL, 128), F32)] * 2,
        compiler_params=params(1),
        cost_estimate=pl.CostEstimate(
            flops=4_000_000_000, bytes_accessed=5_000_000, transcendentals=3_200_000
        ),
        name="attention",
    )(res_len, *slots, short, part, q_gain, k_gain)


def short_kernel(
    dest_ref, move_ref, short_ref, qg_ref, kg_ref, out_ref, gain_ref
):
    slot = lax.axis_index("head")
    move_len = move_ref[find_source(dest_ref, lax.axis_index("dp"))]
    count = WAYS * MOV
    lane = lax.broadcasted_iota(jnp.int32, (1, count), 1)
    bias = jnp.where(lane < move_len, 0.0, -1e30).astype(F32)
    gain_ref[...] = jnp.zeros_like(gain_ref)
    zero = jnp.zeros((WAYS, MOV, 128), F32)

    def rows_at(values, first):
        return values[:, first : first + MOV].reshape(count, 128)

    for head in range(HEADS):
        cols = slice(head * 128, (head + 1) * 128)
        lines = short_ref[:, :, cols].astype(F32)
        q, k, v = rows_at(lines, 0), rows_at(lines, 8), rows_at(lines, 16)
        g = rows_at(lines, 24)
        dq, dk = grads(q.astype(BF16), k.astype(BF16), v.astype(BF16), g.astype(BF16), bias)
        dq = dq.astype(BF16).astype(F32)
        dk = (dk * SCALE).astype(BF16).astype(F32)
        for n, grad, norm, gains in ((0, dq, q, qg_ref), (1, dk, k, kg_ref)):
            both = jnp.concatenate([zero, grad.reshape(WAYS, MOV, 128)], axis=1)
            out_ref[:, n, :, cols] = both.astype(BF16)
            total = jnp.sum(grad * norm, axis=0, keepdims=True)
            total = total / gains[pl.ds(slot * HEADS + head, 1)]
            gain_ref[n * HEADS + head : n * HEADS + head + 1] = total


def short_attention(dest, move_len, short, q_gain, k_gain):
    return pl.pallas_call(
        short_kernel,
        grid=(1,),
        in_specs=[SMEM] * 2 + [whole_block((WAYS, 32, LOCAL))] + [whole_block((BLOCKS, 128))] * 2,
        out_specs=[whole_block((WAYS, 2, 16, LOCAL)), whole_block((8, 128))],
        out_shape=[
            jax.ShapeDtypeStruct((WAYS, 2, 16, LOCAL), BF16),
            jax.ShapeDtypeStruct((8, 128), F32),
        ],
        compiler_params=params(1),
        cost_estimate=pl.CostEstimate(
            flops=20_000_000, bytes_accessed=1_000_000, transcendentals=12_000
        ),
        name="short_attention",
    )(dest, move_len, short, q_gain, k_gain)


POST_ROWS = 64


def post_kernel(q_ref, k_ref, raw_ref, qg_ref, kg_ref, dq_ref, dk_ref, oq_ref, ok_ref):
    last = pl.program_id(0) == TOK_DEV // POST_ROWS - 1
    row = lax.broadcasted_iota(jnp.int32, (POST_ROWS, 1), 0)
    use_short = jnp.logical_and(last, row >= POST_ROWS - MOV)

    def one(in_ref, which, gain_ref, grad_ref, out_ref):
        short = raw_ref[which].astype(F32)
        short = jnp.concatenate([jnp.zeros((POST_ROWS - 16, HD), F32), short], axis=0)
        x = jnp.where(use_short, short, in_ref[...].astype(F32))
        scale = lax.rsqrt(jnp.sum(x * x, axis=1, keepdims=True) / HD + EPS)
        gain = gain_ref[...]
        grad = jnp.concatenate([grad_ref[p, 0].astype(F32) for p in range(WAYS)], axis=1) * gain
        dots = jnp.sum(x * grad, axis=1, keepdims=True)
        out_ref[...] = (scale * grad - x * ((scale * scale * scale) * dots / HD)).astype(BF16)

    one(q_ref, 0, qg_ref, dq_ref, oq_ref)
    one(k_ref, 1, kg_ref, dk_ref, ok_ref)


def finish(q_in, k_in, raw, q_gain, k_gain, back):
    rows = pl.BlockSpec((POST_ROWS, HD), lambda i: (i, 0))
    gain = pl.BlockSpec((1, HD), lambda i: (0, 0))
    return pl.pallas_call(
        post_kernel,
        grid=(TOK_DEV // POST_ROWS,),
        in_specs=[
            rows,
            rows,
            pl.BlockSpec((2, 16, HD), lambda i: (0, 0, 0)),
            gain,
            gain,
            pl.BlockSpec((WAYS, 1, POST_ROWS, LOCAL), lambda i: (0, 0, i, 0)),
            pl.BlockSpec((WAYS, 1, POST_ROWS, LOCAL), lambda i: (0, 1, i, 0)),
        ],
        out_specs=[rows, rows],
        out_shape=[jax.ShapeDtypeStruct((TOK_DEV, HD), BF16)] * 2,
        compiler_params=params(1),
        cost_estimate=pl.CostEstimate(flops=20_000_000, bytes_accessed=4_800_000, transcendentals=0),
        name="finish",
    )(q_in, k_in, raw, q_gain, k_gain, back, back)


EARLY = (4,)
LATE = (6, 1, 3, 5, 2, 7)


def swap_all(x, axis):
    return lax.all_to_all(x, axis, split_axis=0, concat_axis=0, tiled=True)


def gather_sum(x, rings):
    return jnp.sum(lax.all_gather(x, "dp", axis_index_groups=rings), axis=0)


def local(
    q_in, k_in, v_in, grad_out, q_gain, k_gain,
    res_len, move_len, step_index, dest_group, loss_weight,
):
    gain_q, gain_k = q_gain.reshape(1, HD), k_gain.reshape(1, HD)
    steps = step_index.T.reshape(2 * GROUPS)
    packed, grad_rows = lax.optimization_barrier((pack_short(q_in, k_in, v_in), grad_out))
    spread = swap_all(packed, "dp")
    own, *outgoing = prepare(
        dest_group, res_len, move_len, steps, loss_weight,
        q_in, k_in, v_in, grad_rows, gain_q, gain_k,
    )
    slots = {0: own}
    for n in EARLY + LATE:
        slots[n] = lax.ppermute(outgoing[n - 1], "head", [(i, i ^ n) for i in range(WAYS)])
    spread, *held = lax.optimization_barrier((spread, *(slots[n] for n in EARLY)))
    slots.update(zip(EARLY, held, strict=True))
    routed = swap_all(scatter_short(dest_group, spread), "dp")
    short, raw = unpack_short(
        dest_group, move_len, steps, loss_weight, routed, grad_rows, gain_q, gain_k
    )
    short = swap_all(short, "head")
    gain_q_rows, gain_k_rows = q_gain.reshape(BLOCKS, 128), k_gain.reshape(BLOCKS, 128)
    short, part = short_attention(dest_group, move_len, short, gain_q_rows, gain_k_rows)
    grad, part = attention(
        res_len, [slots[n] for n in range(WAYS)], short, part, gain_q_rows, gain_k_rows
    )
    back = swap_all(grad, "head")
    total = gather_sum(gather_sum(part, ZRING), PLANE)
    out_q, out_k = finish(q_in, k_in, raw, gain_q, gain_k, back)
    return (
        out_q,
        out_k,
        total[:HEADS].reshape(LOCAL),
        total[HEADS : 2 * HEADS].reshape(LOCAL),
    )


def solution(mesh):
    tokens = P(("dp", "head"), None)
    return jax.shard_map(
        local,
        mesh=mesh,
        in_specs=(tokens,) * 4 + (P(),) * 7,
        out_specs=(tokens, tokens, P("head"), P("head")),
        check_vma=False,
    )
```
